32 devices in a mesh: groups: 2 (over y), src: 4 (over z), dst: 4 (over x, core).
Axes of the slice: x: 2, y: 2, z: 4, core: 2. Of those that a mesh axis runs over, the one named last changes fastest.
Arguments:
- blocks: bfloat16 [20480, 128, 128], P(('groups', 'src', 'dst')), parts along dimension 0, may hold values from -1 to 1
- block_rows: int32 [20480], P(('groups', 'src', 'dst')), parts along dimension 0, may hold values from 0 to 255, as said below
- block_cols: int32 [20480], P(('groups', 'src', 'dst')), parts along dimension 0, may hold values from 0 to 127, as said below
- row_counts: int32 [65536], P(('groups', 'src')), parts along dimension 0, may hold values from 16 to 5952
- col_counts: int32 [32768], P(('groups', 'dst')), parts along dimension 0, may hold values from 16 to 5952
- start_panel: float32 [32, 32768], P(None, ('groups', 'dst')), parts along dimension 1, may hold values from -30 to 30
Outputs:
- coherent_panel: float32 [32, 32768], P(None, ('groups', 'dst')), parts along dimension 1
The draws below stay inside these ranges and needn't reach their ends.
There are 2 independent parts, one for each index of `groups`. The reference program is written for one: setup_inputs(seed, part) draws one part's arguments, and reference() takes and returns one part's arrays. A program takes and returns all parts, laid end to end along the dimension named above; each array names one. Nothing has to cross between parts.
Inputs may be any that keep to these rules, and one draw needn't show every extreme that they name: `block_rows`: with q = j // 640, s = q // n and d = q % n (n devices along dst), entry j lies in block rows 64 * s to 64 * s + 63; every block row is named by exactly 40 entries, no two of them with the same block column. `block_cols`: with s and d as for block_rows, entry j lies in block columns 32 * d to 32 * d + 31; every block column is named by some entry.
All inputs are finite; a program needn't handle non-finite values.
Results may differ from the reference program's by a relative error of at most 0.0047.
Values may be sent and summed in bfloat16 or wider, within the bound.
No kernel may reach another device: no remote copies, remote signals or barrier semaphores. Data moves between devices by JAX's collectives and lax.ppermute only.
A program may use at most 128 MiB of HBM per device.

```python
import math
import jax
import jax.numpy as jnp
from jax import lax

BOX = 128
PANEL = 32
BPR = 40
ITERS = 2
RBS = 64
CBD = 32
BLK_DEV = 640
NBLK = 10240
NSRC = 32768
NDST = 16384
N_SRC = 4
N_DST = 4


def count_draw(key, count_total):
    mant_key = jax.random.fold_in(key, 5)
    expo_key = jax.random.fold_in(key, 6)
    mantissa = jax.random.randint(mant_key, (count_total,), 16, 32)
    exponent = jax.random.randint(expo_key, (count_total,), 0, 7)
    places = jnp.arange(count_total, dtype=jnp.int32)
    tilted = 192 - 128 * places // count_total
    values = jnp.left_shift(mantissa, exponent) * tilted // 64
    values = jnp.where(places == 0, 5952, values)
    values = jnp.where(places == count_total - 1, 16, values)
    return values.astype(jnp.int32)


def draw_row_counts(key, part):
    return count_draw(jax.random.fold_in(key, 21), NSRC)


def draw_col_counts(key, part):
    return count_draw(jax.random.fold_in(key, 22), NDST)


def block_layout(key):
    rows_key = jax.random.fold_in(key, 31)
    cols_key = jax.random.fold_in(key, 32)
    order_key = jax.random.fold_in(key, 33)
    shifts = jax.vmap(lambda one_key: jax.random.permutation(one_key, RBS))(jax.random.split(rows_key, N_SRC)) % N_DST
    dst_ids = jnp.arange(N_DST, dtype=jnp.int32)
    residue = (dst_ids[None, :, None] - shifts[:, None, :]) % N_DST
    per_row = (BPR - residue + N_DST - 1) // N_DST
    row_ends = jnp.cumsum(per_row, axis=-1).reshape(N_SRC * N_DST, RBS)
    slots = jnp.arange(BLK_DEV, dtype=jnp.int32)
    local_row = jax.vmap(lambda ends: jnp.searchsorted(ends, slots, side='right'))(row_ends).astype(jnp.int32)
    col_perm = jax.vmap(lambda one_key: jax.random.permutation(one_key, CBD))(jax.random.split(cols_key, N_SRC * N_DST))
    local_col = jnp.take(col_perm, slots % CBD, axis=1).astype(jnp.int32)
    orders = jax.vmap(lambda one_key: jax.random.permutation(one_key, BLK_DEV))(jax.random.split(order_key, N_SRC * N_DST))
    local_row = jnp.take_along_axis(local_row, orders, axis=1).reshape(N_SRC, N_DST, BLK_DEV)
    local_col = jnp.take_along_axis(local_col, orders, axis=1).reshape(N_SRC, N_DST, BLK_DEV)
    global_row = local_row + RBS * jnp.arange(N_SRC, dtype=jnp.int32)[:, None, None]
    global_col = local_col + CBD * jnp.arange(N_DST, dtype=jnp.int32)[None, :, None]
    return (global_row.reshape(-1).astype(jnp.int32), global_col.reshape(-1).astype(jnp.int32))


def draw_block_rows(key, part):
    return block_layout(key)[0]


def draw_block_cols(key, part):
    return block_layout(key)[1]


def draw_start_panel(key, part):
    scale_key = jax.random.fold_in(key, 41)
    noise_key = jax.random.fold_in(key, 43)
    column_scale = jnp.exp(jax.random.uniform(scale_key, (PANEL, 1), minval=0.0, maxval=math.log(10.0)))
    values = column_scale * jax.random.truncated_normal(noise_key, -3.0, 3.0, (PANEL, NDST))
    return values.astype(jnp.float32)


def block_scale(key, extent, cuts, least, top_value):
    def one(position, blocks):
        heights = jax.random.uniform(jax.random.fold_in(jax.random.fold_in(key, 6), position), (blocks,), jnp.float32, least / len(cuts), top_value / len(cuts))
        return jnp.repeat(jnp.exp(heights), extent[position] // blocks).reshape((-1,) + (1,) * (len(extent) - position - 1))

    factor_of = one(*cuts[0])
    for cut in cuts[1:]:
        factor_of = factor_of * one(*cut)
    return factor_of


def setup_inputs(seed: int = 0, part: int = 0) -> dict:
    streams_of = jax.random.split(jax.random.key(seed), 7)
    part_splits = jax.random.split(jax.random.fold_in(streams_of[6], part), 7)
    blocks = jnp.clip(jax.random.uniform(part_splits[0], (NBLK, BOX, BOX), jnp.float32, -1.0, 1.0) * block_scale(part_splits[0], (NBLK, BOX, BOX), ((0, 16),), -0.4, 0.0), -1.0, 1.0).astype(jnp.bfloat16)
    block_rows = draw_block_rows(jax.random.fold_in(jax.random.fold_in(streams_of[6], part), 71), part)
    block_cols = draw_block_cols(jax.random.fold_in(jax.random.fold_in(streams_of[6], part), 71), part)
    row_counts = draw_row_counts(jax.random.fold_in(jax.random.fold_in(streams_of[6], part), 71), part)
    col_counts = draw_col_counts(jax.random.fold_in(jax.random.fold_in(streams_of[6], part), 71), part)
    start_panel = draw_start_panel(jax.random.fold_in(jax.random.fold_in(streams_of[6], part), 71), part)
    return {"blocks": blocks, "block_rows": block_rows, "block_cols": block_cols, "row_counts": row_counts, "col_counts": col_counts, "start_panel": start_panel}


def orthonormal(panel_in):
    gram_matrix = jnp.einsum('ckb,clb->kl', panel_in, panel_in, precision=lax.Precision.HIGHEST) / NDST
    factor = jnp.linalg.cholesky(gram_matrix)
    inverse = jax.scipy.linalg.solve_triangular(factor, jnp.eye(PANEL, dtype=jnp.float32), lower=True)
    return jnp.einsum('kl,clb->ckb', inverse, panel_in, precision=lax.Precision.HIGHEST)

def reference(blocks, block_rows, block_cols, row_counts, col_counts, start_panel):
    row_blocks = NSRC // BOX
    col_blocks = NDST // BOX
    step_count = NBLK // BLK_DEV
    row_scale = row_counts.astype(jnp.float32).reshape(row_blocks, 1, BOX)
    col_scale = jnp.sqrt(col_counts.astype(jnp.float32)).reshape(col_blocks, 1, BOX)
    tile_sets = blocks.reshape(step_count, BLK_DEV, BOX, BOX)
    row_sets = block_rows.reshape(step_count, BLK_DEV)
    col_sets = block_cols.reshape(step_count, BLK_DEV)
    current = start_panel.reshape(PANEL, col_blocks, BOX).transpose(1, 0, 2)
    for sweep_index in range(ITERS):
        scaled = (current / col_scale).astype(jnp.bfloat16)

        def forward_step(running, entries):
            tile_group, row_ids, col_ids = entries
            picked = scaled[col_ids].astype(jnp.float32)
            contrib = jnp.einsum('bkj,bij->bki', picked, tile_group.astype(jnp.float32), precision=lax.Precision.HIGHEST)
            return (running.at[row_ids].add(contrib), None)
        product_rows, _ = lax.scan(forward_step, jnp.zeros((row_blocks, PANEL, BOX), jnp.float32), (tile_sets, row_sets, col_sets))
        weighted = (product_rows / row_scale).astype(jnp.bfloat16)

        def adjoint_step(running, entries):
            tile_group, row_ids, col_ids = entries
            picked = weighted[row_ids].astype(jnp.float32)
            contrib = jnp.einsum('bki,bij->bkj', picked, tile_group.astype(jnp.float32), precision=lax.Precision.HIGHEST)
            return (running.at[col_ids].add(contrib), None)
        product_cols, _ = lax.scan(adjoint_step, jnp.zeros((col_blocks, PANEL, BOX), jnp.float32), (tile_sets, row_sets, col_sets))
        current = orthonormal(orthonormal(product_cols / col_scale))
    return current.transpose(1, 0, 2).reshape(PANEL, NDST)
```

```python
import functools

import jax
import jax.numpy as jnp
from jax import lax
from jax.experimental import pallas as pl
from jax.experimental.pallas import tpu as pltpu
from jax.sharding import PartitionSpec as P

ITERS = 2
F32 = jnp.float32
BF16 = jnp.bfloat16
VMEM = pl.BlockSpec(memory_space=pltpu.VMEM)
SMEM = pl.BlockSpec(memory_space=pltpu.SMEM)
ANY = pl.BlockSpec(memory_space=pl.ANY)
LIMIT = 20 << 20


def params():
    return pltpu.CompilerParams(vmem_limit_bytes=LIMIT)


def dot_nn(a, b, precision=None):
    return lax.dot_general(
        a, b, (((1,), (0,)), ((), ())), preferred_element_type=F32, precision=precision
    )


def dot_nt(a, b, precision=None):
    return lax.dot_general(
        a, b, (((1,), (1,)), ((), ())), preferred_element_type=F32, precision=precision
    )


def unroll_of(total):
    for size in (128, 64, 32, 16, 8, 4, 2, 1):
        if total % size == 0:
            return size
    return 1


def add_group(pieces, ids_ref, first, base, accs):
    for t, piece in enumerate(pieces):
        acc = accs[t % len(accs)]
        place = ids_ref[first + t] - base
        acc[place] += piece


def forward_group(panel_ref, cols_ref, col_base, blocks_ref, first, size):
    pieces = []
    side = panel_ref.shape[1]
    for t in range(0, size, 2):
        one = panel_ref[cols_ref[first + t] - col_base]
        two = panel_ref[cols_ref[first + t + 1] - col_base]
        zero = jnp.zeros_like(one)
        left = jnp.concatenate(
            [jnp.concatenate([one, zero], 1), jnp.concatenate([zero, two], 1)], 0
        )
        right = jnp.concatenate([blocks_ref[first + t], blocks_ref[first + t + 1]], 1)
        out = dot_nt(left, right)
        pieces += [out[:side], out[side:]]
    return pieces


def adjoint_group(panel_ref, rows_ref, row_base, blocks_ref, first, size):
    pieces = []
    side, box = panel_ref.shape[1:]
    for t in range(0, size, 2):
        left = jnp.concatenate(
            [
                panel_ref[rows_ref[first + t] - row_base],
                panel_ref[rows_ref[first + t + 1] - row_base],
            ],
            0,
        )
        right = jnp.concatenate([blocks_ref[first + t], blocks_ref[first + t + 1]], 1)
        out = dot_nn(left, right)
        pieces += [out[:side, :box], out[side:, box:]]
    return pieces


def inverse_factor(gram):
    side = gram.shape[0]
    row_ids = lax.broadcasted_iota(jnp.int32, (side, 2 * side), 0)
    col_ids = lax.broadcasted_iota(jnp.int32, (side, 2 * side), 1)
    eye = (col_ids == row_ids + side).astype(F32)
    work = jnp.concatenate([gram, jnp.zeros_like(gram)], 1) + eye
    for j in range(side - 1):
        pivot_row = work[j : j + 1, :]
        scaled_row = pivot_row / work[j : j + 1, j : j + 1]
        column = jnp.where(row_ids[:, :1] > j, work[:, j : j + 1], 0.0)
        work = work - column * scaled_row
    diag = jnp.sum(jnp.where(col_ids == row_ids, work, 0.0), axis=1, keepdims=True)
    return work[:, side:] / jnp.sqrt(diag)


def orth_matrix(gram):
    first = inverse_factor(gram)
    high = lax.Precision.HIGHEST
    again = dot_nt(dot_nn(first, gram, high), first, high)
    return dot_nn(inverse_factor(again), first, high)


def tree_sum(parts):
    while len(parts) > 1:
        parts = [parts[i] + parts[i + 1] for i in range(0, len(parts), 2)]
    return parts[0]


def basis_of(w_ref, gram_refs, box_total):
    gram = tree_sum([g[...] for g in gram_refs]) / box_total
    matrix = orth_matrix(gram)
    top = matrix.astype(BF16)
    rest = matrix - top.astype(F32)
    mid = rest.astype(BF16)
    low = (rest - mid.astype(F32)).astype(BF16)
    side = matrix.shape[0]
    wide = jnp.concatenate([w_ref[c] for c in range(w_ref.shape[0])], 1)
    out = dot_nn(jnp.concatenate([top, mid, low], 0), wide)
    return out[:side] + out[side : 2 * side] + out[2 * side :]


def store_scaled(basis, counts_ref, panel_ref):
    box = panel_ref.shape[2]
    scaled = (basis / jnp.sqrt(counts_ref[...].astype(F32))).astype(BF16)
    for c in range(panel_ref.shape[0]):
        panel_ref[c] = scaled[:, c * box : (c + 1) * box]


def split_halves(accs, core, keep_ref, send_ref):
    half = keep_ref.shape[0]
    mine = pl.ds(core * half, half)
    other = pl.ds((1 - core) * half, half)
    keep_ref[...] = functools.reduce(jnp.add, [a[mine] for a in accs])
    send_ref[...] = functools.reduce(jnp.add, [a[other] for a in accs]).astype(BF16)


def first_forward_kernel(
    unroll, rows_ref, cols_ref, start_ref, counts_ref, hbm_ref,
    keep_ref, send_ref, blocks_ref, panel_ref, acc_a, acc_b, sems,
):
    total = blocks_ref.shape[0]

    def part(i):
        span = pl.ds(i * unroll, unroll)
        return pltpu.make_async_copy(hbm_ref.at[span], blocks_ref.at[span], sems.at[i])

    for i in range(total // unroll):
        part(i).start()
    core = lax.axis_index("dst") % 2
    row_base = lax.axis_index("src") * acc_a.shape[0]
    col_base = lax.axis_index("dst") * panel_ref.shape[0]
    store_scaled(start_ref[...], counts_ref, panel_ref)
    acc_a[...] = jnp.zeros_like(acc_a)
    acc_b[...] = jnp.zeros_like(acc_b)

    def step(i, carry):
        part(i).wait()
        first = i * unroll
        pieces = forward_group(panel_ref, cols_ref, col_base, blocks_ref, first, unroll)
        add_group(pieces, rows_ref, first, row_base, (acc_a, acc_b))
        return carry

    lax.fori_loop(0, total // unroll, step, 0)
    split_halves((acc_a, acc_b), core, keep_ref, send_ref)


def forward_kernel(unroll, box_total, n_gram, rows_ref, cols_ref, counts_ref, blocks_ref, w_ref, *refs):
    gram_refs = refs[:n_gram]
    keep_ref, send_ref, panel_ref, acc_a, acc_b = refs[n_gram:]
    core = lax.axis_index("dst") % 2
    row_base = lax.axis_index("src") * acc_a.shape[0]
    col_base = lax.axis_index("dst") * panel_ref.shape[0]
    store_scaled(basis_of(w_ref, gram_refs, box_total), counts_ref, panel_ref)
    acc_a[...] = jnp.zeros_like(acc_a)
    acc_b[...] = jnp.zeros_like(acc_b)

    def step(i, carry):
        first = i * unroll
        pieces = forward_group(panel_ref, cols_ref, col_base, blocks_ref, first, unroll)
        add_group(pieces, rows_ref, first, row_base, (acc_a, acc_b))
        return carry

    lax.fori_loop(0, blocks_ref.shape[0] // unroll, step, 0)
    split_halves((acc_a, acc_b), core, keep_ref, send_ref)


def adjoint_kernel(unroll, n_src, rows_ref, cols_ref, counts_ref, blocks_ref, mine_ref, other_ref, *refs):
    keep_ref, send_refs = refs[0], refs[1:n_src]
    panel_ref, acc_a, acc_b = refs[n_src:]
    core = lax.axis_index("dst") % 2
    source = lax.axis_index("src")
    row_base = source * panel_ref.shape[0]
    col_base = lax.axis_index("dst") * acc_a.shape[0]
    half = mine_ref.shape[0]
    panel_ref[pl.ds(core * half, half)] = mine_ref[...]
    panel_ref[pl.ds((1 - core) * half, half)] = other_ref[...]
    acc_a[...] = jnp.zeros_like(acc_a)
    acc_b[...] = jnp.zeros_like(acc_b)

    def step(i, carry):
        first = i * unroll
        pieces = adjoint_group(panel_ref, rows_ref, row_base, blocks_ref, first, unroll)
        add_group(pieces, cols_ref, first, col_base, (acc_a, acc_b))
        return carry

    lax.fori_loop(0, blocks_ref.shape[0] // unroll, step, 0)
    size = keep_ref.shape[0]
    for k in range(n_src):
        span = pl.ds((source ^ k) * size, size)
        scale = jnp.sqrt(counts_ref[span].astype(F32))
        value = (acc_a[span] + acc_b[span]) / scale
        if k == 0:
            keep_ref[...] = value
        else:
            send_refs[k - 1][...] = value.astype(BF16)


def gram_kernel(n_src, *refs):
    chunk_refs, (w_ref, gram_ref) = refs[:n_src], refs[n_src:]
    source = lax.axis_index("src")
    size = chunk_refs[0].shape[0]
    for k in range(n_src):
        w_ref[pl.ds((source ^ k) * size, size)] = chunk_refs[k][...]
    wide = jnp.concatenate([w_ref[c] for c in range(w_ref.shape[0])], 1)
    gram_ref[...] = dot_nt(wide, wide)


def basis_kernel(box_total, n_gram, w_ref, *refs):
    refs[n_gram][...] = basis_of(w_ref, refs[:n_gram], box_total)


def swap(x, axis, bits):
    size = lax.axis_size(axis)
    return lax.ppermute(x, axis, [(i, i ^ bits) for i in range(size)])


def per_device(blocks, block_rows, block_cols, row_counts, col_counts, start_panel):
    total, box, _ = blocks.shape
    side = start_panel.shape[0]
    row_blocks = row_counts.shape[0] // box
    col_blocks = col_counts.shape[0] // box
    n_src, n_dst = lax.axis_size("src"), lax.axis_size("dst")
    box_total = float(col_blocks * box * n_dst)
    unroll = unroll_of(total)
    half = row_blocks // 2
    size = col_blocks // n_src
    wide_counts = col_counts.reshape(1, col_blocks * box)
    tall_counts = col_counts.reshape(col_blocks, 1, box)
    core = lax.axis_index("dst") % 2
    row_scale = row_counts.reshape(2, half, 1, box)[core].astype(F32)

    keep_out = jax.ShapeDtypeStruct((half, side, box), F32)
    send_out = jax.ShapeDtypeStruct((half, side, box), BF16)
    forward_scratch = [
        pltpu.VMEM((col_blocks, side, box), BF16),
        pltpu.VMEM((row_blocks, side, box), F32),
        pltpu.VMEM((row_blocks, side, box), F32),
    ]
    held = None
    w_full, grams = None, None
    for sweep in range(ITERS):
        if sweep == 0:
            keep, send, held = pl.pallas_call(
                functools.partial(first_forward_kernel, unroll),
                in_specs=[SMEM, SMEM, VMEM, VMEM, ANY],
                out_specs=[VMEM, VMEM, VMEM],
                out_shape=[keep_out, send_out, pltpu.VMEM(blocks.shape, BF16)],
                scratch_shapes=forward_scratch + [pltpu.SemaphoreType.DMA((total // unroll,))],
                compiler_params=params(),
                name="first_forward",
            )(block_rows, block_cols, start_panel, wide_counts, blocks)
        else:
            keep, send = pl.pallas_call(
                functools.partial(forward_kernel, unroll, box_total, n_dst),
                in_specs=[SMEM, SMEM] + [VMEM] * (3 + n_dst),
                out_specs=[VMEM, VMEM],
                out_shape=[keep_out, send_out],
                scratch_shapes=forward_scratch,
                compiler_params=params(),
                name="forward",
            )(block_rows, block_cols, wide_counts, held, w_full, *grams)
        held = pltpu.with_memory_space_constraint(held, pltpu.VMEM)
        summed = keep + swap(send, "dst", 1).astype(F32)
        bits = 2
        while bits < n_dst:
            summed = summed + swap(summed.astype(BF16), "dst", bits).astype(F32)
            bits *= 2
        mine = (summed / row_scale).astype(BF16)
        other = swap(mine, "dst", 1)
        chunk = (size, side, box)
        outs = pl.pallas_call(
            functools.partial(adjoint_kernel, unroll, n_src),
            in_specs=[SMEM, SMEM] + [VMEM] * 4,
            out_specs=[VMEM] * n_src,
            out_shape=[jax.ShapeDtypeStruct(chunk, F32)]
            + [jax.ShapeDtypeStruct(chunk, BF16)] * (n_src - 1),
            scratch_shapes=[
                pltpu.VMEM((row_blocks, side, box), BF16),
                pltpu.VMEM((col_blocks, side, box), F32),
                pltpu.VMEM((col_blocks, side, box), F32),
            ],
            compiler_params=params(),
            name="adjoint",
        )(block_rows, block_cols, tall_counts, held, mine, other)
        got = [swap(outs[k], "src", k) for k in range(1, n_src)]
        own = tree_sum([outs[0]] + [g.astype(F32) for g in got]).astype(BF16)
        chunks = [own] + [swap(own, "src", k) for k in range(1, n_src)]
        w_full, gram = pl.pallas_call(
            functools.partial(gram_kernel, n_src),
            in_specs=[VMEM] * n_src,
            out_specs=[VMEM, VMEM],
            out_shape=[
                jax.ShapeDtypeStruct((col_blocks, side, box), BF16),
                jax.ShapeDtypeStruct((side, side), F32),
            ],
            compiler_params=params(),
            name="gram",
        )(*chunks)
        grams = [gram] + [swap(gram, "dst", k) for k in range(1, n_dst)]
    return pl.pallas_call(
        functools.partial(basis_kernel, box_total, n_dst),
        in_specs=[VMEM] * (1 + n_dst),
        out_specs=VMEM,
        out_shape=jax.ShapeDtypeStruct((side, col_blocks * box), F32),
        compiler_params=params(),
        name="basis",
    )(w_full, *grams)


def solution(mesh):
    return jax.shard_map(
        per_device,
        mesh=mesh,
        in_specs=(
            P(("groups", "src", "dst"), None, None),
            P(("groups", "src", "dst")),
            P(("groups", "src", "dst")),
            P(("groups", "src")),
            P(("groups", "dst")),
            P(None, ("groups", "dst")),
        ),
        out_specs=P(None, ("groups", "dst")),
        check_vma=False,
    )
```

```python
import functools

import jax
import jax.numpy as jnp
from jax import lax
from jax.experimental import pallas as pl
from jax.experimental.pallas import tpu as pltpu
from jax.sharding import PartitionSpec as P

ITERS = 2
F32 = jnp.float32
BF16 = jnp.bfloat16
VMEM = pl.BlockSpec(memory_space=pltpu.VMEM)
SMEM = pl.BlockSpec(memory_space=pltpu.SMEM)
HBM = pl.BlockSpec(memory_space=pltpu.HBM)


def cost(flops, moved=0):
    return pl.CostEstimate(flops=flops, bytes_accessed=moved, transcendentals=0)


def params(mebibytes=6):
    return pltpu.CompilerParams(vmem_limit_bytes=mebibytes << 20)


def dot_nn(a, b, precision=None):
    return lax.dot_general(
        a, b, (((1,), (0,)), ((), ())), preferred_element_type=F32, precision=precision
    )


def dot_nt(a, b, precision=None):
    return lax.dot_general(
        a, b, (((1,), (1,)), ((), ())), preferred_element_type=F32, precision=precision
    )


def unroll_of(total):
    for size in (128, 64, 32, 16, 8, 4, 2, 1):
        if total % size == 0:
            return size
    return 1


def add_group(pieces, ids_ref, first, base, accs):
    for t, piece in enumerate(pieces):
        acc = accs[t % len(accs)]
        place = ids_ref[first + t] - base
        acc[place] += piece


def forward_group(panel_ref, cols_ref, col_base, blocks_ref, first, start, size):
    pieces = []
    side = panel_ref.shape[1]
    for t in range(0, size, 2):
        one = panel_ref[cols_ref[first + t] - col_base]
        two = panel_ref[cols_ref[first + t + 1] - col_base]
        zero = jnp.zeros_like(one)
        left = jnp.concatenate(
            [jnp.concatenate([one, zero], 1), jnp.concatenate([zero, two], 1)], 0
        )
        right = jnp.concatenate([blocks_ref[start + t], blocks_ref[start + t + 1]], 1)
        out = dot_nt(left, right)
        pieces += [out[:side], out[side:]]
    return pieces


def adjoint_group(panel_ref, rows_ref, row_base, blocks_ref, first, size):
    pieces = []
    side, box = panel_ref.shape[1:]
    for t in range(0, size, 2):
        left = jnp.concatenate(
            [
                panel_ref[rows_ref[first + t] - row_base],
                panel_ref[rows_ref[first + t + 1] - row_base],
            ],
            0,
        )
        right = jnp.concatenate([blocks_ref[first + t], blocks_ref[first + t + 1]], 1)
        out = dot_nn(left, right)
        pieces += [out[:side, :box], out[side:, box:]]
    return pieces


def inverse_factor(gram):
    side = gram.shape[0]
    row_ids = lax.broadcasted_iota(jnp.int32, (side, 2 * side), 0)
    col_ids = lax.broadcasted_iota(jnp.int32, (side, 2 * side), 1)
    eye = (col_ids == row_ids + side).astype(F32)
    work = jnp.concatenate([gram, jnp.zeros_like(gram)], 1) + eye
    for j in range(side - 1):
        pivot_row = work[j : j + 1, :]
        scaled_row = pivot_row / work[j : j + 1, j : j + 1]
        column = jnp.where(row_ids[:, :1] > j, work[:, j : j + 1], 0.0)
        work = work - column * scaled_row
    diag = jnp.sum(jnp.where(col_ids == row_ids, work, 0.0), axis=1, keepdims=True)
    return work[:, side:] / jnp.sqrt(diag)


def orth_matrix(gram):
    first = inverse_factor(gram)
    high = lax.Precision.HIGHEST
    again = dot_nt(dot_nn(first, gram, high), first, high)
    return dot_nn(inverse_factor(again), first, high)


def tree_sum(parts):
    while len(parts) > 1:
        parts = [parts[i] + parts[i + 1] for i in range(0, len(parts), 2)]
    return parts[0]


def split3(x):
    top = x.astype(BF16)
    rest = x - top.astype(F32)
    mid = rest.astype(BF16)
    return top, mid, (rest - mid.astype(F32)).astype(BF16)


def orth_of(gram_refs, box_total):
    return orth_matrix(tree_sum([g[...] for g in gram_refs]) / box_total)


def store_scaled(basis, counts_ref, panel_ref):
    box = panel_ref.shape[2]
    scaled = (basis / jnp.sqrt(counts_ref[...].astype(F32))).astype(BF16)
    for c in range(panel_ref.shape[0]):
        panel_ref[c] = scaled[:, c * box : (c + 1) * box]


def split_halves(accs, core, keep_ref, send_ref):
    half = keep_ref.shape[0]
    mine = pl.ds(core * half, half)
    other = pl.ds((1 - core) * half, half)
    keep_ref[...] = functools.reduce(jnp.add, [a[mine] for a in accs])
    send_ref[...] = functools.reduce(jnp.add, [a[other] for a in accs]).astype(BF16)


def first_forward_kernel(
    unroll, rows_hbm, cols_hbm, start_hbm, counts_hbm, blocks_hbm,
    keep_ref, send_ref,
    rows_ref, cols_ref, start_ref, counts_ref, blocks_ref, panel_ref, acc_a, acc_b, sems, small_sems,
):
    steps = blocks_hbm.shape[0] // unroll
    slots = blocks_ref.shape[0]

    def part(i, slot):
        return pltpu.make_async_copy(
            blocks_hbm.at[pl.ds(i * unroll, unroll)], blocks_ref.at[slot], sems.at[slot]
        )

    small = [
        pltpu.make_async_copy(source, target, small_sems.at[i])
        for i, (source, target) in enumerate(
            (
                (start_hbm, start_ref),
                (counts_hbm, counts_ref),
                (rows_hbm, rows_ref),
                (cols_hbm, cols_ref),
            )
        )
    ]
    for copy in small:
        copy.start()
    for i in range(min(slots, steps)):
        part(i, i).start()
    row_base = lax.axis_index("src") * acc_a.shape[0]
    col_base = lax.axis_index("dst") * panel_ref.shape[0]
    acc_a[...] = jnp.zeros_like(acc_a)
    acc_b[...] = jnp.zeros_like(acc_b)
    for copy in small:
        copy.wait()
    store_scaled(start_ref[...], counts_ref, panel_ref)

    def step(i, carry):
        slot = lax.rem(i, slots)
        part(i, slot).wait()
        pieces = forward_group(panel_ref, cols_ref, col_base, blocks_ref.at[slot], i * unroll, 0, unroll)
        add_group(pieces, rows_ref, i * unroll, row_base, (acc_a, acc_b))

        @pl.when(i + slots < steps)
        def _():
            part(i + slots, slot).start()

        return carry

    lax.fori_loop(0, steps, step, 0)
    split_halves((acc_a, acc_b), lax.axis_index("dst") % 2, keep_ref, send_ref)


def load_kernel(hbm_ref, held_ref, sem):
    copy = pltpu.make_async_copy(hbm_ref, held_ref, sem)
    copy.start()
    copy.wait()


def forward_kernel(unroll, rows_ref, cols_ref, blocks_ref, panel_ref, keep_ref, send_ref, acc_a, acc_b):
    row_base = lax.axis_index("src") * acc_a.shape[0]
    col_base = lax.axis_index("dst") * panel_ref.shape[0]
    acc_a[...] = jnp.zeros_like(acc_a)
    acc_b[...] = jnp.zeros_like(acc_b)

    def step(i, carry):
        first = i * unroll
        pieces = forward_group(panel_ref, cols_ref, col_base, blocks_ref, first, first, unroll)
        add_group(pieces, rows_ref, first, row_base, (acc_a, acc_b))
        return carry

    lax.fori_loop(0, blocks_ref.shape[0] // unroll, step, 0)
    split_halves((acc_a, acc_b), lax.axis_index("dst") % 2, keep_ref, send_ref)


def adjoint_kernel(unroll, n_src, rows_ref, cols_ref, counts_ref, blocks_ref, mine_ref, other_ref, *refs):
    keep_ref, send_refs = refs[0], refs[1:n_src]
    panel_ref, acc_a, acc_b = refs[n_src:]
    core = lax.axis_index("dst") % 2
    source = lax.axis_index("src")
    row_base = source * panel_ref.shape[0]
    col_base = lax.axis_index("dst") * acc_a.shape[0]
    half = mine_ref.shape[0]
    panel_ref[pl.ds(core * half, half)] = mine_ref[...]
    panel_ref[pl.ds((1 - core) * half, half)] = other_ref[...]
    acc_a[...] = jnp.zeros_like(acc_a)
    acc_b[...] = jnp.zeros_like(acc_b)

    def step(i, carry):
        first = i * unroll
        pieces = adjoint_group(panel_ref, rows_ref, row_base, blocks_ref, first, unroll)
        add_group(pieces, cols_ref, first, col_base, (acc_a, acc_b))
        return carry

    lax.fori_loop(0, blocks_ref.shape[0] // unroll, step, 0)
    size = keep_ref.shape[0]
    for k in range(n_src):
        span = pl.ds((source ^ k) * size, size)
        scale = jnp.sqrt(counts_ref[span].astype(F32))
        value = (acc_a[span] + acc_b[span]) / scale
        if k == 0:
            keep_ref[...] = value
        else:
            send_refs[k - 1][...] = value.astype(BF16)


def gram_kernel(n_src, last, counts_ref, *refs):
    chunk_refs, (w_ref, gram_ref) = refs[:n_src], refs[n_src:]
    source = lax.axis_index("src")
    size = chunk_refs[0].shape[0]
    for k in range(n_src):
        w_ref[pl.ds((source ^ k) * size, size)] = chunk_refs[k][...]
    wide = jnp.concatenate([w_ref[c] for c in range(w_ref.shape[0])], 1)
    gram_ref[...] = dot_nt(wide, wide)
    if not last:
        w_ref[...] = (w_ref[...].astype(F32) / jnp.sqrt(counts_ref[...].astype(F32))).astype(BF16)


def orth_kernel(box_total, *refs):
    refs[-1][...] = orth_of(refs[:-1], box_total)


def basis_kernel(box_total, w_ref, *refs):
    matrix = orth_of(refs[:-1], box_total)
    side = matrix.shape[0]
    wide = jnp.concatenate([w_ref[c] for c in range(w_ref.shape[0])], 1)
    out = dot_nn(jnp.concatenate(split3(matrix), 0), wide)
    refs[-1][...] = out[:side] + out[side : 2 * side] + out[2 * side :]


def mix_kernel(matrix_ref, scale_ref, keep_ref, core_ref, *refs):
    out_ref = refs[-1]
    half, side, box = out_ref.shape
    total = keep_ref[...] + core_ref[...].astype(F32)
    for ref in refs[:-1]:
        total = total + ref[...].astype(F32)
    wide = jnp.concatenate([total[c] for c in range(half)], 1)
    top, mid, low = split3(wide)
    left = split3(matrix_ref[...])
    one = dot_nn(jnp.concatenate(left, 0), top)
    two = dot_nn(jnp.concatenate(left[:2], 0), mid)
    three = dot_nn(left[0], low)
    mixed = one[:side] + (one[side : 2 * side] + two[:side]) + (one[2 * side :] + two[side:] + three)
    for c in range(half):
        out_ref[c] = (mixed[:, c * box : (c + 1) * box] / scale_ref[c].astype(F32)).astype(BF16)


def swap(x, axis, bits):
    size = lax.axis_size(axis)
    return lax.ppermute(x, axis, [(i, i ^ bits) for i in range(size)])


def per_device(blocks, block_rows, block_cols, row_counts, col_counts, start_panel):
    total, box, _ = blocks.shape
    side = start_panel.shape[0]
    row_blocks = row_counts.shape[0] // box
    col_blocks = col_counts.shape[0] // box
    n_src, n_dst = lax.axis_size("src"), lax.axis_size("dst")
    box_total = float(col_blocks * box * n_dst)
    unroll = unroll_of(total)
    half = row_blocks // 2
    size = col_blocks // n_src
    wide_counts = col_counts.reshape(1, col_blocks * box)
    tall_counts = col_counts.reshape(col_blocks, 1, box)
    core = lax.axis_index("dst") % 2
    row_scale = row_counts.reshape(2, half, 1, box)[core]
    forward_cost = cost(2 * total * box * box * 512)
    adjoint_cost = cost(2 * total * box * box * 256)
    small_cost = cost(1 << 28)
    orth_cost = cost(1 << 32)

    keep_out = jax.ShapeDtypeStruct((half, side, box), F32)
    send_out = jax.ShapeDtypeStruct((half, side, box), BF16)
    square = jax.ShapeDtypeStruct((side, side), F32)
    accs = [pltpu.VMEM((row_blocks, side, box), F32)] * 2
    w_full, grams = None, None
    for sweep in range(ITERS):
        if sweep == 0:
            slots = min(total // unroll, 3)
            keep, send = pl.pallas_call(
                functools.partial(first_forward_kernel, unroll),
                in_specs=[HBM] * 5,
                out_specs=[VMEM, VMEM],
                out_shape=[keep_out, send_out],
                scratch_shapes=[
                    pltpu.SMEM(block_rows.shape, jnp.int32),
                    pltpu.SMEM(block_cols.shape, jnp.int32),
                    pltpu.VMEM(start_panel.shape, F32),
                    pltpu.VMEM(wide_counts.shape, jnp.int32),
                    pltpu.VMEM((slots, unroll, box, box), BF16),
                    pltpu.VMEM((col_blocks, side, box), BF16),
                    *accs,
                    pltpu.SemaphoreType.DMA((slots,)),
                    pltpu.SemaphoreType.DMA((4,)),
                ],
                compiler_params=params(18),
                name="first_forward",
                cost_estimate=forward_cost,
            )(*[
                pltpu.with_memory_space_constraint(x, pltpu.HBM)
                for x in (block_rows, block_cols, start_panel, wide_counts, blocks)
            ])
        else:
            keep, send = pl.pallas_call(
                functools.partial(forward_kernel, unroll),
                in_specs=[SMEM, SMEM, VMEM, VMEM],
                out_specs=[VMEM, VMEM],
                out_shape=[keep_out, send_out],
                scratch_shapes=accs,
                compiler_params=params(),
                name="forward",
                cost_estimate=forward_cost,
            )(block_rows, block_cols, held, w_full)
        core_got = swap(send, "dst", 1)
        if sweep == 0:
            again, core_got = lax.optimization_barrier((blocks, core_got))
            held = pl.pallas_call(
                load_kernel,
                in_specs=[HBM],
                out_specs=VMEM,
                out_shape=pltpu.VMEM(blocks.shape, BF16),
                scratch_shapes=[pltpu.SemaphoreType.DMA],
                compiler_params=params(2),
                name="load",
                cost_estimate=cost(0, 2 * total * box * box * 2),
            )(pltpu.with_memory_space_constraint(again, pltpu.HBM))
        summed = keep + core_got.astype(F32)
        x_got = []
        bits = 2
        while bits < n_dst:
            x_got.append(swap(summed.astype(BF16), "dst", bits))
            summed = summed + x_got[-1].astype(F32)
            bits *= 2
        if sweep == 0:
            summed, held = lax.optimization_barrier((summed, held))
            mine = (summed / row_scale.astype(F32)).astype(BF16)
        else:
            matrix = pl.pallas_call(
                functools.partial(orth_kernel, box_total),
                in_specs=[VMEM] * n_dst,
                out_specs=VMEM,
                out_shape=square,
                compiler_params=params(),
                name="orth",
                cost_estimate=orth_cost,
            )(*grams)
            mine = pl.pallas_call(
                mix_kernel,
                in_specs=[VMEM] * (4 + len(x_got)),
                out_specs=VMEM,
                out_shape=send_out,
                compiler_params=params(),
                name="mix",
                cost_estimate=small_cost,
            )(matrix, row_scale, keep, core_got, *x_got)
        other = swap(mine, "dst", 1)
        chunk = (size, side, box)
        outs = pl.pallas_call(
            functools.partial(adjoint_kernel, unroll, n_src),
            in_specs=[SMEM, SMEM] + [VMEM] * 4,
            out_specs=[VMEM] * n_src,
            out_shape=[jax.ShapeDtypeStruct(chunk, F32)]
            + [jax.ShapeDtypeStruct(chunk, BF16)] * (n_src - 1),
            scratch_shapes=[
                pltpu.VMEM((row_blocks, side, box), BF16),
                pltpu.VMEM((col_blocks, side, box), F32),
                pltpu.VMEM((col_blocks, side, box), F32),
            ],
            compiler_params=params(),
            name="adjoint",
                cost_estimate=adjoint_cost,
        )(block_rows, block_cols, tall_counts, held, mine, other)
        got = [swap(outs[k], "src", k) for k in range(1, n_src)]
        own = tree_sum([outs[0]] + [g.astype(F32) for g in got]).astype(BF16)
        chunks = [own] + [swap(own, "src", k) for k in range(1, n_src)]
        w_full, gram = pl.pallas_call(
            functools.partial(gram_kernel, n_src, sweep == ITERS - 1),
            in_specs=[VMEM] * (1 + n_src),
            out_specs=[VMEM, VMEM],
            out_shape=[jax.ShapeDtypeStruct((col_blocks, side, box), BF16), square],
            compiler_params=params(),
            name="gram",
                cost_estimate=small_cost,
        )(tall_counts, *chunks)
        grams = [gram] + [swap(gram, "dst", k) for k in range(1, n_dst)]
    return pl.pallas_call(
        functools.partial(basis_kernel, box_total),
        in_specs=[VMEM] * (1 + n_dst),
        out_specs=VMEM,
        out_shape=jax.ShapeDtypeStruct((side, col_blocks * box), F32),
        compiler_params=params(),
        name="basis",
                cost_estimate=orth_cost,
    )(w_full, *grams)


def solution(mesh):
    return jax.shard_map(
        per_device,
        mesh=mesh,
        in_specs=(
            P(("groups", "src", "dst"), None, None),
            P(("groups", "src", "dst")),
            P(("groups", "src", "dst")),
            P(("groups", "src")),
            P(("groups", "dst")),
            P(None, ("groups", "dst")),
        ),
        out_specs=P(None, ("groups", "dst")),
        check_vma=False,
    )
```

```python
import functools

import jax
import jax.numpy as jnp
from jax import lax
from jax.experimental import pallas as pl
from jax.experimental.pallas import tpu as pltpu
from jax.sharding import PartitionSpec as P

ITERS = 2
TURNED = 3
F32 = jnp.float32
BF16 = jnp.bfloat16
VMEM = pl.BlockSpec(memory_space=pltpu.VMEM)
SMEM = pl.BlockSpec(memory_space=pltpu.SMEM)
HBM = pl.BlockSpec(memory_space=pltpu.HBM)


def cost(flops, moved=0):
    return pl.CostEstimate(flops=flops, bytes_accessed=moved, transcendentals=0)


def params(mebibytes=6):
    return pltpu.CompilerParams(vmem_limit_bytes=mebibytes << 20)


def dot_nn(a, b, precision=None):
    return lax.dot_general(
        a, b, (((1,), (0,)), ((), ())), preferred_element_type=F32, precision=precision
    )


def dot_nt(a, b, precision=None):
    return lax.dot_general(
        a, b, (((1,), (1,)), ((), ())), preferred_element_type=F32, precision=precision
    )


def unroll_of(total, most):
    while total % most:
        most //= 2
    return most


def add_group(pieces, ids_ref, first, base, accs):
    for t, piece in enumerate(pieces):
        acc = accs[t % len(accs)]
        place = ids_ref[first + t] - base
        acc[place] += piece


def forward_group(panel_ref, cols_ref, col_base, block_at, first, size):
    pieces = []
    side, box = panel_ref.shape[1:]
    for t in range(0, size, 2):
        left = jnp.concatenate(
            [
                panel_ref[cols_ref[first + t] - col_base],
                panel_ref[cols_ref[first + t + 1] - col_base],
            ],
            0,
        )
        out = dot_nn(left, jnp.concatenate([block_at(t), block_at(t + 1)], 1))
        pieces += [out[:side, :box], out[side:, box:]]
    return pieces


def adjoint_group(panel_ref, rows_ref, row_base, held_ref, first, size):
    pieces = []
    side, box = panel_ref.shape[1:]
    for t in range(0, size, 2):
        left = jnp.concatenate(
            [
                panel_ref[rows_ref[first + t] - row_base],
                panel_ref[rows_ref[first + t + 1] - row_base],
            ],
            0,
        )
        right = jnp.concatenate([held_ref[first + t], held_ref[first + t + 1]], 1)
        out = dot_nn(left, right)
        pieces += [out[:side, :box], out[side:, box:]]
    return pieces


def inverse_factor(gram):
    side = gram.shape[0]
    row = lax.broadcasted_iota(jnp.int32, (side, 2 * side), 0)
    col = lax.broadcasted_iota(jnp.int32, (side, 2 * side), 1)
    work = jnp.concatenate([gram, jnp.zeros_like(gram)], 1) + (col == row + side).astype(F32)
    for j in range(0, side, 4):
        column = [jnp.broadcast_to(work[:, j + k : j + k + 1], work.shape) for k in range(4)]
        r0, r1, r2, r3 = [work[j + k : j + k + 1, :] for k in range(4)]
        at = [[column[k][j + i : j + i + 1, :] for k in range(4)] for i in range(4)]
        a, b, c = at[0][0], at[1][0], at[1][1]
        inv = 1.0 / (a * c - b * b)
        ia, ib, ic = c * inv, -b * inv, a * inv
        t0, t1 = ia * r0 + ib * r1, ib * r0 + ic * r1
        p0, p1, q0, q1 = at[2][0], at[2][1], at[3][0], at[3][1]
        gp0, gp1 = ia * p0 + ib * p1, ib * p0 + ic * p1
        gq0, gq1 = ia * q0 + ib * q1, ib * q0 + ic * q1
        sa = at[2][2] - (p0 * gp0 + p1 * gp1)
        sb = at[3][2] - (q0 * gp0 + q1 * gp1)
        sc = at[3][3] - (q0 * gq0 + q1 * gq1)
        n1 = r1 - (b / a) * r0
        n2 = r2 - (p0 * t0 + p1 * t1)
        n3 = r3 - (q0 * t0 + q1 * t1)
        inv_s = 1.0 / (sa * sc - sb * sb)
        u0, u1 = (sc * n2 - sb * n3) * inv_s, (sa * n3 - sb * n2) * inv_s
        v0, v1 = t0 - (gp0 * u0 + gq0 * u1), t1 - (gp1 * u0 + gq1 * u1)
        below = work - ((column[0] * v0 + column[1] * v1) + (column[2] * u0 + column[3] * u1))
        work = jnp.where(row > j + 3, below, work)
        for k, new in ((1, n1), (2, n2), (3, n3 - (sb / sa) * n2)):
            work = jnp.where(row == j + k, new, work)
    diag = jnp.sum(jnp.where(col == row, work, 0.0), axis=1, keepdims=True)
    return work[:, side:] / jnp.sqrt(diag)


def orth_matrix(gram):
    first = inverse_factor(gram)
    high = lax.Precision.HIGHEST
    again = dot_nt(dot_nn(first, gram, high), first, high)
    return dot_nn(inverse_factor(again), first, high)


def tree_sum(parts):
    while len(parts) > 1:
        parts = [parts[i] + parts[i + 1] for i in range(0, len(parts), 2)]
    return parts[0]


def split3(x):
    top = x.astype(BF16)
    rest = x - top.astype(F32)
    mid = rest.astype(BF16)
    return top, mid, (rest - mid.astype(F32)).astype(BF16)


def orth_of(gram_refs, box_total):
    return orth_matrix(tree_sum([g[...] for g in gram_refs]) / box_total)


def store_scaled(basis, counts_ref, panel_ref):
    box = panel_ref.shape[2]
    scaled = (basis / jnp.sqrt(counts_ref[...].astype(F32))).astype(BF16)
    for c in range(panel_ref.shape[0]):
        panel_ref[c] = scaled[:, c * box : (c + 1) * box]


def split_halves(accs, core, keep_ref, send_ref):
    half = keep_ref.shape[0]
    mine = pl.ds(core * half, half)
    other = pl.ds((1 - core) * half, half)
    keep_ref[...] = functools.reduce(jnp.add, [a[mine] for a in accs])
    send_ref[...] = functools.reduce(jnp.add, [a[other] for a in accs]).astype(BF16)


def first_forward_kernel(
    unroll, rows_hbm, cols_hbm, start_hbm, counts_hbm, blocks_hbm,
    keep_ref, send_ref,
    rows_ref, cols_ref, start_ref, counts_ref, blocks_ref, panel_ref, acc_a, acc_b, sems, small_sems,
):
    steps = blocks_hbm.shape[0] // unroll
    slots = blocks_ref.shape[0]

    def part(i, slot):
        return pltpu.make_async_copy(
            blocks_hbm.at[pl.ds(i * unroll, unroll)], blocks_ref.at[slot], sems.at[slot]
        )

    small = [
        pltpu.make_async_copy(source, target, small_sems.at[i])
        for i, (source, target) in enumerate(
            (
                (start_hbm, start_ref),
                (counts_hbm, counts_ref),
                (rows_hbm, rows_ref),
                (cols_hbm, cols_ref),
            )
        )
    ]
    for copy in small:
        copy.start()
    for i in range(min(slots, steps)):
        part(i, i).start()
    row_base = lax.axis_index("src") * acc_a.shape[0]
    col_base = lax.axis_index("dst") * panel_ref.shape[0]
    acc_a[...] = jnp.zeros_like(acc_a)
    acc_b[...] = jnp.zeros_like(acc_b)
    for copy in small:
        copy.wait()
    store_scaled(start_ref[...], counts_ref, panel_ref)

    def step(i, carry):
        slot = lax.rem(i, slots)
        part(i, slot).wait()
        pieces = forward_group(
            panel_ref, cols_ref, col_base, lambda t: blocks_ref[slot, t].T, i * unroll, unroll
        )
        add_group(pieces, rows_ref, i * unroll, row_base, (acc_a, acc_b))

        @pl.when(i + slots < steps)
        def _():
            part(i + slots, slot).start()

        return carry

    lax.fori_loop(0, steps, step, 0)
    split_halves((acc_a, acc_b), lax.axis_index("dst") % 2, keep_ref, send_ref)


def load_kernel(unroll, turned, hbm_ref, held_ref, sems):
    total = hbm_ref.shape[0]
    steps = total // unroll

    def part(i):
        span = pl.ds(i * unroll, unroll)
        return pltpu.make_async_copy(hbm_ref.at[span], held_ref.at[span], sems.at[i])

    for i in range(steps):
        part(i).start()

    for i in range(steps):
        part(i).wait()
        for t in range(turned):
            held_ref[total + i * turned + t] = held_ref[i * unroll + t].T


def forward_kernel(unroll, turned, rows_ref, cols_ref, held_ref, panel_ref, keep_ref, send_ref, acc_a, acc_b):
    total = rows_ref.shape[0]
    row_base = lax.axis_index("src") * acc_a.shape[0]
    col_base = lax.axis_index("dst") * panel_ref.shape[0]
    acc_a[...] = jnp.zeros_like(acc_a)
    acc_b[...] = jnp.zeros_like(acc_b)

    def step(i, carry):
        first = i * unroll

        def block_at(t):
            if t < turned:
                return held_ref[total + i * turned + t]
            return held_ref[first + t].T

        pieces = forward_group(panel_ref, cols_ref, col_base, block_at, first, unroll)
        add_group(pieces, rows_ref, first, row_base, (acc_a, acc_b))
        return carry

    lax.fori_loop(0, total // unroll, step, 0)
    split_halves((acc_a, acc_b), lax.axis_index("dst") % 2, keep_ref, send_ref)


def adjoint_kernel(unroll, n_src, rows_ref, cols_ref, counts_ref, held_ref, mine_ref, other_ref, *refs):
    keep_ref, send_refs = refs[0], refs[1:n_src]
    panel_ref, acc_a, acc_b = refs[n_src:]
    core = lax.axis_index("dst") % 2
    source = lax.axis_index("src")
    row_base = source * panel_ref.shape[0]
    col_base = lax.axis_index("dst") * acc_a.shape[0]
    half = mine_ref.shape[0]
    panel_ref[pl.ds(core * half, half)] = mine_ref[...]
    panel_ref[pl.ds((1 - core) * half, half)] = other_ref[...]
    acc_a[...] = jnp.zeros_like(acc_a)
    acc_b[...] = jnp.zeros_like(acc_b)

    def step(i, carry):
        first = i * unroll
        pieces = adjoint_group(panel_ref, rows_ref, row_base, held_ref, first, unroll)
        add_group(pieces, cols_ref, first, col_base, (acc_a, acc_b))
        return carry

    lax.fori_loop(0, rows_ref.shape[0] // unroll, step, 0)
    size = keep_ref.shape[0]
    for k in range(n_src):
        span = pl.ds((source ^ k) * size, size)
        scale = jnp.sqrt(counts_ref[span].astype(F32))
        value = (acc_a[span] + acc_b[span]) / scale
        if k == 0:
            keep_ref[...] = value
        else:
            send_refs[k - 1][...] = value.astype(BF16)


def gram_kernel(n_src, last, counts_ref, *refs):
    chunk_refs, (w_ref, gram_ref) = refs[:n_src], refs[n_src:]
    source = lax.axis_index("src")
    size = chunk_refs[0].shape[0]
    for k in range(n_src):
        w_ref[pl.ds((source ^ k) * size, size)] = chunk_refs[k][...]
    wide = jnp.concatenate([w_ref[c] for c in range(w_ref.shape[0])], 1)
    gram_ref[...] = dot_nt(wide, wide)
    if not last:
        w_ref[...] = (w_ref[...].astype(F32) / jnp.sqrt(counts_ref[...].astype(F32))).astype(BF16)


def orth_kernel(box_total, *refs):
    refs[-1][...] = orth_of(refs[:-1], box_total)


def basis_kernel(box_total, w_ref, *refs):
    matrix = orth_of(refs[:-1], box_total)
    side = matrix.shape[0]
    wide = jnp.concatenate([w_ref[c] for c in range(w_ref.shape[0])], 1)
    out = dot_nn(jnp.concatenate(split3(matrix), 0), wide)
    refs[-1][...] = out[:side] + out[side : 2 * side] + out[2 * side :]


def mix_kernel(matrix_ref, scale_ref, keep_ref, core_ref, *refs):
    out_ref = refs[-1]
    half, side, box = out_ref.shape
    total = keep_ref[...] + core_ref[...].astype(F32)
    for ref in refs[:-1]:
        total = total + ref[...].astype(F32)
    wide = jnp.concatenate([total[c] for c in range(half)], 1)
    top, mid, low = split3(wide)
    left = split3(matrix_ref[...])
    one = dot_nn(jnp.concatenate(left, 0), top)
    two = dot_nn(jnp.concatenate(left[:2], 0), mid)
    three = dot_nn(left[0], low)
    mixed = one[:side] + (one[side : 2 * side] + two[:side]) + (one[2 * side :] + two[side:] + three)
    for c in range(half):
        out_ref[c] = (mixed[:, c * box : (c + 1) * box] / scale_ref[c].astype(F32)).astype(BF16)


def swap(x, axis, bits):
    size = lax.axis_size(axis)
    return lax.ppermute(x, axis, [(i, i ^ bits) for i in range(size)])


def per_device(blocks, block_rows, block_cols, row_counts, col_counts, start_panel):
    total, box, _ = blocks.shape
    side = start_panel.shape[0]
    row_blocks = row_counts.shape[0] // box
    col_blocks = col_counts.shape[0] // box
    n_src, n_dst = lax.axis_size("src"), lax.axis_size("dst")
    box_total = float(col_blocks * box * n_dst)
    unroll = unroll_of(total, 128)
    turned = unroll * TURNED // 8
    half = row_blocks // 2
    size = col_blocks // n_src
    wide_counts = col_counts.reshape(1, col_blocks * box)
    tall_counts = col_counts.reshape(col_blocks, 1, box)
    core = lax.axis_index("dst") % 2
    row_scale = row_counts.reshape(2, half, 1, box)[core]
    forward_cost = cost(2 * total * box * box * 512)
    adjoint_cost = cost(2 * total * box * box * 256)
    small_cost = cost(1 << 28)
    orth_cost = cost(1 << 32)

    keep_out = jax.ShapeDtypeStruct((half, side, box), F32)
    send_out = jax.ShapeDtypeStruct((half, side, box), BF16)
    square = jax.ShapeDtypeStruct((side, side), F32)
    accs = [pltpu.VMEM((row_blocks, side, box), F32)] * 2
    w_full, grams = None, None
    for sweep in range(ITERS):
        if sweep == 0:
            slots = min(total // unroll, 3)
            keep, send = pl.pallas_call(
                functools.partial(first_forward_kernel, unroll),
                in_specs=[HBM] * 5,
                out_specs=[VMEM, VMEM],
                out_shape=[keep_out, send_out],
                scratch_shapes=[
                    pltpu.SMEM(block_rows.shape, jnp.int32),
                    pltpu.SMEM(block_cols.shape, jnp.int32),
                    pltpu.VMEM(start_panel.shape, F32),
                    pltpu.VMEM(wide_counts.shape, jnp.int32),
                    pltpu.VMEM((slots, unroll, box, box), BF16),
                    pltpu.VMEM((col_blocks, side, box), BF16),
                    *accs,
                    pltpu.SemaphoreType.DMA((slots,)),
                    pltpu.SemaphoreType.DMA((4,)),
                ],
                compiler_params=params(18),
                name="first_forward",
                cost_estimate=forward_cost,
            )(*[
                pltpu.with_memory_space_constraint(x, pltpu.HBM)
                for x in (block_rows, block_cols, start_panel, wide_counts, blocks)
            ])
        else:
            keep, send = pl.pallas_call(
                functools.partial(forward_kernel, unroll, turned),
                in_specs=[SMEM, SMEM, VMEM, VMEM],
                out_specs=[VMEM, VMEM],
                out_shape=[keep_out, send_out],
                scratch_shapes=accs,
                compiler_params=params(),
                name="forward",
                cost_estimate=forward_cost,
            )(block_rows, block_cols, held, w_full)
        core_got = swap(send, "dst", 1)
        if sweep == 0:
            again, core_got = lax.optimization_barrier((blocks, core_got))
            held = pl.pallas_call(
                functools.partial(load_kernel, unroll, turned),
                in_specs=[HBM],
                out_specs=VMEM,
                out_shape=pltpu.VMEM((total + total // unroll * turned, box, box), BF16),
                scratch_shapes=[pltpu.SemaphoreType.DMA((total // unroll,))],
                compiler_params=params(2),
                name="load",
                cost_estimate=cost(0, 2 * total * box * box * 2),
            )(pltpu.with_memory_space_constraint(again, pltpu.HBM))
        summed = keep + core_got.astype(F32)
        x_got = []
        bits = 2
        while bits < n_dst:
            x_got.append(swap(summed.astype(BF16), "dst", bits))
            summed = summed + x_got[-1].astype(F32)
            bits *= 2
        if sweep == 0:
            summed, held = lax.optimization_barrier((summed, held))
            mine = (summed / row_scale.astype(F32)).astype(BF16)
        else:
            matrix = pl.pallas_call(
                functools.partial(orth_kernel, box_total),
                in_specs=[VMEM] * n_dst,
                out_specs=VMEM,
                out_shape=square,
                compiler_params=params(),
                name="orth",
                cost_estimate=orth_cost,
            )(*grams)
            mine = pl.pallas_call(
                mix_kernel,
                in_specs=[VMEM] * (4 + len(x_got)),
                out_specs=VMEM,
                out_shape=send_out,
                compiler_params=params(),
                name="mix",
                cost_estimate=small_cost,
            )(matrix, row_scale, keep, core_got, *x_got)
        other = swap(mine, "dst", 1)
        chunk = (size, side, box)
        outs = pl.pallas_call(
            functools.partial(adjoint_kernel, unroll, n_src),
            in_specs=[SMEM, SMEM] + [VMEM] * 4,
            out_specs=[VMEM] * n_src,
            out_shape=[jax.ShapeDtypeStruct(chunk, F32)]
            + [jax.ShapeDtypeStruct(chunk, BF16)] * (n_src - 1),
            scratch_shapes=[
                pltpu.VMEM((row_blocks, side, box), BF16),
                pltpu.VMEM((col_blocks, side, box), F32),
                pltpu.VMEM((col_blocks, side, box), F32),
            ],
            compiler_params=params(),
            name="adjoint",
                cost_estimate=adjoint_cost,
        )(block_rows, block_cols, tall_counts, held, mine, other)
        got = [swap(outs[k], "src", k) for k in range(1, n_src)]
        own = tree_sum([outs[0]] + [g.astype(F32) for g in got]).astype(BF16)
        chunks = [own] + [swap(own, "src", k) for k in range(1, n_src)]
        w_full, gram = pl.pallas_call(
            functools.partial(gram_kernel, n_src, sweep == ITERS - 1),
            in_specs=[VMEM] * (1 + n_src),
            out_specs=[VMEM, VMEM],
            out_shape=[jax.ShapeDtypeStruct((col_blocks, side, box), BF16), square],
            compiler_params=params(),
            name="gram",
                cost_estimate=small_cost,
        )(tall_counts, *chunks)
        grams = [gram] + [swap(gram, "dst", k) for k in range(1, n_dst)]
    return pl.pallas_call(
        functools.partial(basis_kernel, box_total),
        in_specs=[VMEM] * (1 + n_dst),
        out_specs=VMEM,
        out_shape=jax.ShapeDtypeStruct((side, col_blocks * box), F32),
        compiler_params=params(),
        name="basis",
                cost_estimate=orth_cost,
    )(w_full, *grams)


def solution(mesh):
    return jax.shard_map(
        per_device,
        mesh=mesh,
        in_specs=(
            P(("groups", "src", "dst"), None, None),
            P(("groups", "src", "dst")),
            P(("groups", "src", "dst")),
            P(("groups", "src")),
            P(("groups", "dst")),
            P(None, ("groups", "dst")),
        ),
        out_specs=P(None, ("groups", "dst")),
        check_vma=False,
    )
```

```python
import functools

import jax
import jax.numpy as jnp
from jax import lax
from jax.experimental import pallas as pl
from jax.experimental.pallas import tpu as pltpu
from jax.sharding import PartitionSpec as P

ITERS = 2
TURNED = 3
FIRST = 128
SLOTS = 3
MIX = 8
F32 = jnp.float32
BF16 = jnp.bfloat16
VMEM = pl.BlockSpec(memory_space=pltpu.VMEM)
SMEM = pl.BlockSpec(memory_space=pltpu.SMEM)
HBM = pl.BlockSpec(memory_space=pltpu.HBM)


def cost(flops, moved=0):
    return pl.CostEstimate(flops=flops, bytes_accessed=moved, transcendentals=0)


def params(mebibytes=6):
    return pltpu.CompilerParams(vmem_limit_bytes=mebibytes << 20)


def dot_nn(a, b, precision=None):
    return lax.dot_general(
        a, b, (((1,), (0,)), ((), ())), preferred_element_type=F32, precision=precision
    )


def dot_nt(a, b, precision=None):
    return lax.dot_general(
        a, b, (((1,), (1,)), ((), ())), preferred_element_type=F32, precision=precision
    )


def unroll_of(total, most):
    while total % most:
        most //= 2
    return most


def add_group(pieces, ids_ref, first, base, accs):
    for t, piece in enumerate(pieces):
        acc = accs[t % len(accs)]
        place = ids_ref[first + t] - base
        acc[place] += piece


def forward_group(panel_ref, cols_ref, col_base, block_at, plain, first, size):
    pieces = []
    side, box = panel_ref.shape[1:]
    for t in range(0, size, 2):
        left = jnp.concatenate(
            [
                panel_ref[cols_ref[first + t] - col_base],
                panel_ref[cols_ref[first + t + 1] - col_base],
            ],
            0,
        )
        one, two = block_at(t), block_at(t + 1)
        if plain(t):
            out = dot_nt(left, jnp.concatenate([one, two], 0))
        else:
            out = dot_nn(left, jnp.concatenate([one, two], 1))
        pieces += [out[:side, :box], out[side:, box:]]
    return pieces


def adjoint_group(panel_ref, rows_ref, row_base, held_ref, first, size):
    pieces = []
    side, box = panel_ref.shape[1:]
    for t in range(0, size, 2):
        left = jnp.concatenate(
            [
                panel_ref[rows_ref[first + t] - row_base],
                panel_ref[rows_ref[first + t + 1] - row_base],
            ],
            0,
        )
        right = jnp.concatenate([held_ref[first + t], held_ref[first + t + 1]], 1)
        out = dot_nn(left, right)
        pieces += [out[:side, :box], out[side:, box:]]
    return pieces


def inverse_factor(gram):
    side = gram.shape[0]
    row = lax.broadcasted_iota(jnp.int32, (side, 2 * side), 0)
    col = lax.broadcasted_iota(jnp.int32, (side, 2 * side), 1)
    work = jnp.concatenate([gram, jnp.zeros_like(gram)], 1) + (col == row + side).astype(F32)
    for j in range(0, side, 4):
        column = [jnp.broadcast_to(work[:, j + k : j + k + 1], work.shape) for k in range(4)]
        r0, r1, r2, r3 = [work[j + k : j + k + 1, :] for k in range(4)]
        at = [[column[k][j + i : j + i + 1, :] for k in range(4)] for i in range(4)]
        a, b, c = at[0][0], at[1][0], at[1][1]
        inv = 1.0 / (a * c - b * b)
        ia, ib, ic = c * inv, -b * inv, a * inv
        t0, t1 = ia * r0 + ib * r1, ib * r0 + ic * r1
        p0, p1, q0, q1 = at[2][0], at[2][1], at[3][0], at[3][1]
        gp0, gp1 = ia * p0 + ib * p1, ib * p0 + ic * p1
        gq0, gq1 = ia * q0 + ib * q1, ib * q0 + ic * q1
        sa = at[2][2] - (p0 * gp0 + p1 * gp1)
        sb = at[3][2] - (q0 * gp0 + q1 * gp1)
        sc = at[3][3] - (q0 * gq0 + q1 * gq1)
        n1 = r1 - (b / a) * r0
        n2 = r2 - (p0 * t0 + p1 * t1)
        n3 = r3 - (q0 * t0 + q1 * t1)
        inv_s = 1.0 / (sa * sc - sb * sb)
        u0, u1 = (sc * n2 - sb * n3) * inv_s, (sa * n3 - sb * n2) * inv_s
        v0, v1 = t0 - (gp0 * u0 + gq0 * u1), t1 - (gp1 * u0 + gq1 * u1)
        below = work - ((column[0] * v0 + column[1] * v1) + (column[2] * u0 + column[3] * u1))
        work = jnp.where(row > j + 3, below, work)
        for k, new in ((1, n1), (2, n2), (3, n3 - (sb / sa) * n2)):
            work = jnp.where(row == j + k, new, work)
    diag = jnp.sum(jnp.where(col == row, work, 0.0), axis=1, keepdims=True)
    return work[:, side:] / jnp.sqrt(diag)


def orth_matrix(gram):
    first = inverse_factor(gram)
    high = lax.Precision.HIGHEST
    again = dot_nt(dot_nn(first, gram, high), first, high)
    return dot_nn(inverse_factor(again), first, high)


def tree_sum(parts):
    while len(parts) > 1:
        parts = [parts[i] + parts[i + 1] for i in range(0, len(parts), 2)]
    return parts[0]


def split3(x):
    top = x.astype(BF16)
    rest = x - top.astype(F32)
    mid = rest.astype(BF16)
    return top, mid, (rest - mid.astype(F32)).astype(BF16)


def orth_of(gram_refs, box_total):
    return orth_matrix(tree_sum([g[...] for g in gram_refs]) / box_total)


def store_scaled(basis, counts_ref, panel_ref):
    box = panel_ref.shape[2]
    scaled = (basis / jnp.sqrt(counts_ref[...].astype(F32))).astype(BF16)
    for c in range(panel_ref.shape[0]):
        panel_ref[c] = scaled[:, c * box : (c + 1) * box]


def split_halves(accs, core, keep_ref, send_ref):
    half = keep_ref.shape[0]
    mine = pl.ds(core * half, half)
    other = pl.ds((1 - core) * half, half)
    keep_ref[...] = functools.reduce(jnp.add, [a[mine] for a in accs])
    send_ref[...] = functools.reduce(jnp.add, [a[other] for a in accs]).astype(BF16)


def first_forward_kernel(
    unroll, rows_hbm, cols_hbm, start_hbm, counts_hbm, blocks_hbm,
    keep_ref, send_ref,
    rows_ref, cols_ref, start_ref, counts_ref, blocks_ref, panel_ref, acc_a, acc_b, sems, small_sems,
):
    steps = blocks_hbm.shape[0] // unroll
    slots = blocks_ref.shape[0]

    def part(i, slot):
        return pltpu.make_async_copy(
            blocks_hbm.at[pl.ds(i * unroll, unroll)], blocks_ref.at[slot], sems.at[slot]
        )

    small = [
        pltpu.make_async_copy(source, target, small_sems.at[i])
        for i, (source, target) in enumerate(
            (
                (start_hbm, start_ref),
                (counts_hbm, counts_ref),
                (rows_hbm, rows_ref),
                (cols_hbm, cols_ref),
            )
        )
    ]
    for copy in small:
        copy.start()
    for i in range(min(slots, steps)):
        part(i, i).start()
    row_base = lax.axis_index("src") * acc_a.shape[0]
    col_base = lax.axis_index("dst") * panel_ref.shape[0]
    acc_a[...] = jnp.zeros_like(acc_a)
    acc_b[...] = jnp.zeros_like(acc_b)
    for copy in small:
        copy.wait()
    store_scaled(start_ref[...], counts_ref, panel_ref)

    def step(i, carry):
        slot = lax.rem(i, slots)
        part(i, slot).wait()

        def plain(t):
            return t % MIX == MIX - 2

        def block_at(t):
            block = blocks_ref[slot, t]
            return block if plain(t // 2 * 2) else block.T

        pieces = forward_group(
            panel_ref, cols_ref, col_base, block_at, plain, i * unroll, unroll
        )
        add_group(pieces, rows_ref, i * unroll, row_base, (acc_a, acc_b))

        @pl.when(i + slots < steps)
        def _():
            part(i + slots, slot).start()

        return carry

    lax.fori_loop(0, steps, step, 0)
    split_halves((acc_a, acc_b), lax.axis_index("dst") % 2, keep_ref, send_ref)


def load_kernel(hbm_ref, held_ref, sem):
    copy = pltpu.make_async_copy(hbm_ref, held_ref, sem)
    copy.start()
    copy.wait()


def turn_kernel(unroll, turned, held_ref, turned_ref):
    for i in range(turned_ref.shape[0] // turned):
        for t in range(turned):
            turned_ref[i * turned + t] = held_ref[i * unroll + t].T


def forward_kernel(unroll, turned, rows_ref, cols_ref, held_ref, turned_ref, panel_ref, keep_ref, send_ref, acc_a, acc_b):
    total = rows_ref.shape[0]
    row_base = lax.axis_index("src") * acc_a.shape[0]
    col_base = lax.axis_index("dst") * panel_ref.shape[0]
    acc_a[...] = jnp.zeros_like(acc_a)
    acc_b[...] = jnp.zeros_like(acc_b)

    def step(i, carry):
        first = i * unroll

        def block_at(t):
            if t < turned:
                return turned_ref[i * turned + t]
            return held_ref[first + t].T

        pieces = forward_group(panel_ref, cols_ref, col_base, block_at, lambda t: False, first, unroll)
        add_group(pieces, rows_ref, first, row_base, (acc_a, acc_b))
        return carry

    lax.fori_loop(0, total // unroll, step, 0)
    split_halves((acc_a, acc_b), lax.axis_index("dst") % 2, keep_ref, send_ref)


def adjoint_kernel(unroll, n_src, rows_ref, cols_ref, counts_ref, held_ref, mine_ref, other_ref, *refs):
    keep_ref, send_refs = refs[0], refs[1:n_src]
    panel_ref, acc_a, acc_b = refs[n_src:]
    core = lax.axis_index("dst") % 2
    source = lax.axis_index("src")
    row_base = source * panel_ref.shape[0]
    col_base = lax.axis_index("dst") * acc_a.shape[0]
    half = mine_ref.shape[0]
    panel_ref[pl.ds(core * half, half)] = mine_ref[...]
    panel_ref[pl.ds((1 - core) * half, half)] = other_ref[...]
    acc_a[...] = jnp.zeros_like(acc_a)
    acc_b[...] = jnp.zeros_like(acc_b)

    def step(i, carry):
        first = i * unroll
        pieces = adjoint_group(panel_ref, rows_ref, row_base, held_ref, first, unroll)
        add_group(pieces, cols_ref, first, col_base, (acc_a, acc_b))
        return carry

    lax.fori_loop(0, rows_ref.shape[0] // unroll, step, 0)
    size = keep_ref.shape[0]
    for k in range(n_src):
        span = pl.ds((source ^ k) * size, size)
        scale = jnp.sqrt(counts_ref[span].astype(F32))
        value = (acc_a[span] + acc_b[span]) / scale
        if k == 0:
            keep_ref[...] = value
        else:
            send_refs[k - 1][...] = value.astype(BF16)


def gram_kernel(n_src, last, counts_ref, *refs):
    chunk_refs, (w_ref, gram_ref) = refs[:n_src], refs[n_src:]
    source = lax.axis_index("src")
    size = chunk_refs[0].shape[0]
    for k in range(n_src):
        w_ref[pl.ds((source ^ k) * size, size)] = chunk_refs[k][...]
    wide = jnp.concatenate([w_ref[c] for c in range(w_ref.shape[0])], 1)
    gram_ref[...] = dot_nt(wide, wide)
    if not last:
        w_ref[...] = (w_ref[...].astype(F32) / jnp.sqrt(counts_ref[...].astype(F32))).astype(BF16)


def orth_kernel(box_total, *refs):
    refs[-1][...] = orth_of(refs[:-1], box_total)


def basis_kernel(box_total, w_ref, *refs):
    matrix = orth_of(refs[:-1], box_total)
    side = matrix.shape[0]
    wide = jnp.concatenate([w_ref[c] for c in range(w_ref.shape[0])], 1)
    out = dot_nn(jnp.concatenate(split3(matrix), 0), wide)
    refs[-1][...] = out[:side] + out[side : 2 * side] + out[2 * side :]


def mix_kernel(matrix_ref, scale_ref, keep_ref, core_ref, *refs):
    out_ref = refs[-1]
    half, side, box = out_ref.shape
    total = keep_ref[...] + core_ref[...].astype(F32)
    for ref in refs[:-1]:
        total = total + ref[...].astype(F32)
    wide = jnp.concatenate([total[c] for c in range(half)], 1)
    top, mid, low = split3(wide)
    left = split3(matrix_ref[...])
    one = dot_nn(jnp.concatenate(left, 0), top)
    two = dot_nn(jnp.concatenate(left[:2], 0), mid)
    three = dot_nn(left[0], low)
    mixed = one[:side] + (one[side : 2 * side] + two[:side]) + (one[2 * side :] + two[side:] + three)
    for c in range(half):
        out_ref[c] = (mixed[:, c * box : (c + 1) * box] / scale_ref[c].astype(F32)).astype(BF16)


def swap(x, axis, bits):
    size = lax.axis_size(axis)
    return lax.ppermute(x, axis, [(i, i ^ bits) for i in range(size)])


def per_device(blocks, block_rows, block_cols, row_counts, col_counts, start_panel):
    total, box, _ = blocks.shape
    side = start_panel.shape[0]
    row_blocks = row_counts.shape[0] // box
    col_blocks = col_counts.shape[0] // box
    n_src, n_dst = lax.axis_size("src"), lax.axis_size("dst")
    box_total = float(col_blocks * box * n_dst)
    unroll = unroll_of(total, 128)
    first_unroll = unroll_of(total, FIRST)
    turned = unroll * TURNED // 8
    half = row_blocks // 2
    size = col_blocks // n_src
    wide_counts = col_counts.reshape(1, col_blocks * box)
    tall_counts = col_counts.reshape(col_blocks, 1, box)
    core = lax.axis_index("dst") % 2
    row_scale = row_counts.reshape(2, half, 1, box)[core]
    forward_cost = cost(2 * total * box * box * 512)
    adjoint_cost = cost(2 * total * box * box * 256)
    small_cost = cost(1 << 28)
    orth_cost = cost(1 << 32)

    keep_out = jax.ShapeDtypeStruct((half, side, box), F32)
    send_out = jax.ShapeDtypeStruct((half, side, box), BF16)
    square = jax.ShapeDtypeStruct((side, side), F32)
    accs = [pltpu.VMEM((row_blocks, side, box), F32)] * 2
    w_full, grams = None, None
    for sweep in range(ITERS):
        if sweep == 0:
            slots = min(total // first_unroll, SLOTS)
            keep, send = pl.pallas_call(
                functools.partial(first_forward_kernel, first_unroll),
                in_specs=[HBM] * 5,
                out_specs=[VMEM, VMEM],
                out_shape=[keep_out, send_out],
                scratch_shapes=[
                    pltpu.SMEM(block_rows.shape, jnp.int32),
                    pltpu.SMEM(block_cols.shape, jnp.int32),
                    pltpu.VMEM(start_panel.shape, F32),
                    pltpu.VMEM(wide_counts.shape, jnp.int32),
                    pltpu.VMEM((slots, first_unroll, box, box), BF16),
                    pltpu.VMEM((col_blocks, side, box), BF16),
                    *accs,
                    pltpu.SemaphoreType.DMA((slots,)),
                    pltpu.SemaphoreType.DMA((4,)),
                ],
                compiler_params=params(22),
                name="first_forward",
                cost_estimate=forward_cost,
            )(*[
                pltpu.with_memory_space_constraint(x, pltpu.HBM)
                for x in (block_rows, block_cols, start_panel, wide_counts, blocks)
            ])
        else:
            keep, send = pl.pallas_call(
                functools.partial(forward_kernel, unroll, turned),
                in_specs=[SMEM, SMEM, VMEM, VMEM, VMEM],
                out_specs=[VMEM, VMEM],
                out_shape=[keep_out, send_out],
                scratch_shapes=accs,
                compiler_params=params(),
                name="forward",
                cost_estimate=forward_cost,
            )(block_rows, block_cols, held, flipped, w_full)
        core_got = swap(send, "dst", 1)
        if sweep == 0:
            again, core_got = lax.optimization_barrier((blocks, core_got))
            held = pl.pallas_call(
                load_kernel,
                in_specs=[HBM],
                out_specs=VMEM,
                out_shape=pltpu.VMEM(blocks.shape, BF16),
                scratch_shapes=[pltpu.SemaphoreType.DMA],
                compiler_params=params(2),
                name="load",
                cost_estimate=cost(0, 2 * total * box * box * 2),
            )(pltpu.with_memory_space_constraint(again, pltpu.HBM))
        summed = keep + core_got.astype(F32)
        x_got = []
        bits = 2
        while bits < n_dst:
            x_got.append(swap(summed.astype(BF16), "dst", bits))
            summed = summed + x_got[-1].astype(F32)
            bits *= 2
        if sweep == 0:
            summed, held = lax.optimization_barrier((summed, held))
            mine = (summed / row_scale.astype(F32)).astype(BF16)
        else:
            matrix = pl.pallas_call(
                functools.partial(orth_kernel, box_total),
                in_specs=[VMEM] * n_dst,
                out_specs=VMEM,
                out_shape=square,
                compiler_params=params(),
                name="orth",
                cost_estimate=orth_cost,
            )(*grams)
            mine = pl.pallas_call(
                mix_kernel,
                in_specs=[VMEM] * (4 + len(x_got)),
                out_specs=VMEM,
                out_shape=send_out,
                compiler_params=params(),
                name="mix",
                cost_estimate=small_cost,
            )(matrix, row_scale, keep, core_got, *x_got)
        other = swap(mine, "dst", 1)
        chunk = (size, side, box)
        outs = pl.pallas_call(
            functools.partial(adjoint_kernel, unroll, n_src),
            in_specs=[SMEM, SMEM] + [VMEM] * 4,
            out_specs=[VMEM] * n_src,
            out_shape=[jax.ShapeDtypeStruct(chunk, F32)]
            + [jax.ShapeDtypeStruct(chunk, BF16)] * (n_src - 1),
            scratch_shapes=[
                pltpu.VMEM((row_blocks, side, box), BF16),
                pltpu.VMEM((col_blocks, side, box), F32),
                pltpu.VMEM((col_blocks, side, box), F32),
            ],
            compiler_params=params(),
            name="adjoint",
                cost_estimate=adjoint_cost,
        )(block_rows, block_cols, tall_counts, held, mine, other)
        outs = list(outs)
        got = [swap(outs[k], "src", k) for k in range(1, n_src)]
        if sweep == 0:
            outs[0], again = lax.optimization_barrier((outs[0], held))
            flipped = pl.pallas_call(
                functools.partial(turn_kernel, unroll, turned),
                in_specs=[VMEM],
                out_specs=VMEM,
                out_shape=pltpu.VMEM((total // unroll * turned, box, box), BF16),
                compiler_params=params(2),
                name="turn",
                cost_estimate=adjoint_cost,
            )(again)
            got, flipped = lax.optimization_barrier((got, flipped))
        own = tree_sum([outs[0]] + [g.astype(F32) for g in got]).astype(BF16)
        chunks = [own] + [swap(own, "src", k) for k in range(1, n_src)]
        w_full, gram = pl.pallas_call(
            functools.partial(gram_kernel, n_src, sweep == ITERS - 1),
            in_specs=[VMEM] * (1 + n_src),
            out_specs=[VMEM, VMEM],
            out_shape=[jax.ShapeDtypeStruct((col_blocks, side, box), BF16), square],
            compiler_params=params(),
            name="gram",
                cost_estimate=small_cost,
        )(tall_counts, *chunks)
        grams = [gram] + [swap(gram, "dst", k) for k in range(1, n_dst)]
    return pl.pallas_call(
        functools.partial(basis_kernel, box_total),
        in_specs=[VMEM] * (1 + n_dst),
        out_specs=VMEM,
        out_shape=jax.ShapeDtypeStruct((side, col_blocks * box), F32),
        compiler_params=params(),
        name="basis",
                cost_estimate=orth_cost,
    )(w_full, *grams)


def solution(mesh):
    return jax.shard_map(
        per_device,
        mesh=mesh,
        in_specs=(
            P(("groups", "src", "dst"), None, None),
            P(("groups", "src", "dst")),
            P(("groups", "src", "dst")),
            P(("groups", "src")),
            P(("groups", "dst")),
            P(None, ("groups", "dst")),
        ),
        out_specs=P(None, ("groups", "dst")),
        check_vma=False,
    )
```

```python
import functools

import jax
import jax.numpy as jnp
from jax import lax
from jax.experimental import pallas as pl
from jax.experimental.pallas import tpu as pltpu
from jax.sharding import PartitionSpec as P

ITERS = 2
TURNED = 3
FIRST = 128
SECOND = 160
BACK = 320
SLOTS = 3
MIX = 8
F32 = jnp.float32
BF16 = jnp.bfloat16
VMEM = pl.BlockSpec(memory_space=pltpu.VMEM)
SMEM = pl.BlockSpec(memory_space=pltpu.SMEM)
HBM = pl.BlockSpec(memory_space=pltpu.HBM)


def cost(flops, moved=0):
    return pl.CostEstimate(flops=flops, bytes_accessed=moved, transcendentals=0)


def params(mebibytes=6):
    return pltpu.CompilerParams(vmem_limit_bytes=mebibytes << 20)


def dot_nn(a, b, precision=None):
    return lax.dot_general(
        a, b, (((1,), (0,)), ((), ())), preferred_element_type=F32, precision=precision
    )


def dot_nt(a, b, precision=None):
    return lax.dot_general(
        a, b, (((1,), (1,)), ((), ())), preferred_element_type=F32, precision=precision
    )


def unroll_of(total, most):
    return max(size for size in range(8, most + 1, 8) if total % size == 0)


def add_group(pieces, ids_ref, first, base, accs):
    for t, piece in enumerate(pieces):
        acc = accs[t % len(accs)]
        place = ids_ref[first + t] - base
        acc[place] += piece


def forward_group(panel_ref, cols_ref, col_base, block_at, plain, first, size):
    pieces = []
    side, box = panel_ref.shape[1:]
    for t in range(0, size, 2):
        left = jnp.concatenate(
            [
                panel_ref[cols_ref[first + t] - col_base],
                panel_ref[cols_ref[first + t + 1] - col_base],
            ],
            0,
        )
        one, two = block_at(t), block_at(t + 1)
        if plain(t):
            out = dot_nt(left, jnp.concatenate([one, two], 0))
        else:
            out = dot_nn(left, jnp.concatenate([one, two], 1))
        pieces += [out[:side, :box], out[side:, box:]]
    return pieces


def adjoint_group(panel_ref, rows_ref, row_base, held_ref, first, size):
    pieces = []
    side, box = panel_ref.shape[1:]
    for t in range(0, size, 2):
        left = jnp.concatenate(
            [
                panel_ref[rows_ref[first + t] - row_base],
                panel_ref[rows_ref[first + t + 1] - row_base],
            ],
            0,
        )
        right = jnp.concatenate([held_ref[first + t], held_ref[first + t + 1]], 1)
        out = dot_nn(left, right)
        pieces += [out[:side, :box], out[side:, box:]]
    return pieces


def inverse_factor(gram):
    side = gram.shape[0]
    row = lax.broadcasted_iota(jnp.int32, (side, 2 * side), 0)
    col = lax.broadcasted_iota(jnp.int32, (side, 2 * side), 1)
    work = jnp.concatenate([gram, jnp.zeros_like(gram)], 1) + (col == row + side).astype(F32)
    for j in range(0, side, 4):
        column = [jnp.broadcast_to(work[:, j + k : j + k + 1], work.shape) for k in range(4)]
        r0, r1, r2, r3 = [work[j + k : j + k + 1, :] for k in range(4)]
        at = [[column[k][j + i : j + i + 1, :] for k in range(4)] for i in range(4)]
        a, b, c = at[0][0], at[1][0], at[1][1]
        inv = 1.0 / (a * c - b * b)
        ia, ib, ic = c * inv, -b * inv, a * inv
        t0, t1 = ia * r0 + ib * r1, ib * r0 + ic * r1
        p0, p1, q0, q1 = at[2][0], at[2][1], at[3][0], at[3][1]
        gp0, gp1 = ia * p0 + ib * p1, ib * p0 + ic * p1
        gq0, gq1 = ia * q0 + ib * q1, ib * q0 + ic * q1
        sa = at[2][2] - (p0 * gp0 + p1 * gp1)
        sb = at[3][2] - (q0 * gp0 + q1 * gp1)
        sc = at[3][3] - (q0 * gq0 + q1 * gq1)
        n1 = r1 - (b / a) * r0
        n2 = r2 - (p0 * t0 + p1 * t1)
        n3 = r3 - (q0 * t0 + q1 * t1)
        inv_s = 1.0 / (sa * sc - sb * sb)
        u0, u1 = (sc * n2 - sb * n3) * inv_s, (sa * n3 - sb * n2) * inv_s
        v0, v1 = t0 - (gp0 * u0 + gq0 * u1), t1 - (gp1 * u0 + gq1 * u1)
        below = work - ((column[0] * v0 + column[1] * v1) + (column[2] * u0 + column[3] * u1))
        work = jnp.where(row > j + 3, below, work)
        for k, new in ((1, n1), (2, n2), (3, n3 - (sb / sa) * n2)):
            work = jnp.where(row == j + k, new, work)
    diag = jnp.sum(jnp.where(col == row, work, 0.0), axis=1, keepdims=True)
    return work[:, side:] / jnp.sqrt(diag)


def orth_matrix(gram):
    first = inverse_factor(gram)
    high = lax.Precision.HIGHEST
    again = dot_nt(dot_nn(first, gram, high), first, high)
    return dot_nn(inverse_factor(again), first, high)


def tree_sum(parts):
    while len(parts) > 1:
        parts = [parts[i] + parts[i + 1] for i in range(0, len(parts), 2)]
    return parts[0]


def split3(x):
    top = x.astype(BF16)
    rest = x - top.astype(F32)
    mid = rest.astype(BF16)
    return top, mid, (rest - mid.astype(F32)).astype(BF16)


def orth_of(gram_refs, box_total):
    return orth_matrix(tree_sum([g[...] for g in gram_refs]) / box_total)


def store_scaled(basis, counts_ref, panel_ref):
    box = panel_ref.shape[2]
    scaled = (basis / jnp.sqrt(counts_ref[...].astype(F32))).astype(BF16)
    for c in range(panel_ref.shape[0]):
        panel_ref[c] = scaled[:, c * box : (c + 1) * box]


def split_halves(accs, core, keep_ref, send_ref):
    half = keep_ref.shape[0]
    mine = pl.ds(core * half, half)
    other = pl.ds((1 - core) * half, half)
    keep_ref[...] = functools.reduce(jnp.add, [a[mine] for a in accs])
    send_ref[...] = functools.reduce(jnp.add, [a[other] for a in accs]).astype(BF16)


def first_forward_kernel(
    unroll, rows_hbm, cols_hbm, start_hbm, counts_hbm, blocks_hbm,
    keep_ref, send_ref,
    rows_ref, cols_ref, start_ref, counts_ref, blocks_ref, panel_ref, acc_a, acc_b, sems, small_sems,
):
    steps = blocks_hbm.shape[0] // unroll
    slots = blocks_ref.shape[0]

    def part(i, slot):
        return pltpu.make_async_copy(
            blocks_hbm.at[pl.ds(i * unroll, unroll)], blocks_ref.at[slot], sems.at[slot]
        )

    small = [
        pltpu.make_async_copy(source, target, small_sems.at[i])
        for i, (source, target) in enumerate(
            (
                (start_hbm, start_ref),
                (counts_hbm, counts_ref),
                (rows_hbm, rows_ref),
                (cols_hbm, cols_ref),
            )
        )
    ]
    for copy in small:
        copy.start()
    for i in range(min(slots, steps)):
        part(i, i).start()
    row_base = lax.axis_index("src") * acc_a.shape[0]
    col_base = lax.axis_index("dst") * panel_ref.shape[0]
    acc_a[...] = jnp.zeros_like(acc_a)
    acc_b[...] = jnp.zeros_like(acc_b)
    for copy in small:
        copy.wait()
    store_scaled(start_ref[...], counts_ref, panel_ref)

    def step(i, carry):
        slot = lax.rem(i, slots)
        part(i, slot).wait()

        def plain(t):
            return t % MIX == MIX - 2

        def block_at(t):
            block = blocks_ref[slot, t]
            return block if plain(t // 2 * 2) else block.T

        pieces = forward_group(
            panel_ref, cols_ref, col_base, block_at, plain, i * unroll, unroll
        )
        add_group(pieces, rows_ref, i * unroll, row_base, (acc_a, acc_b))

        @pl.when(i + slots < steps)
        def _():
            part(i + slots, slot).start()

        return carry

    lax.fori_loop(0, steps, step, 0)
    split_halves((acc_a, acc_b), lax.axis_index("dst") % 2, keep_ref, send_ref)


def load_kernel(hbm_ref, held_ref, sem):
    copy = pltpu.make_async_copy(hbm_ref, held_ref, sem)
    copy.start()
    copy.wait()


def turn_kernel(unroll, turned, held_ref, turned_ref):
    for i in range(turned_ref.shape[0] // turned):
        for t in range(turned):
            turned_ref[i * turned + t] = held_ref[i * unroll + t].T


def forward_kernel(unroll, turned, rows_ref, cols_ref, held_ref, turned_ref, panel_ref, keep_ref, send_ref, acc_a, acc_b):
    total = rows_ref.shape[0]
    row_base = lax.axis_index("src") * acc_a.shape[0]
    col_base = lax.axis_index("dst") * panel_ref.shape[0]
    acc_a[...] = jnp.zeros_like(acc_a)
    acc_b[...] = jnp.zeros_like(acc_b)

    def step(i, carry):
        first = i * unroll

        def block_at(t):
            if t < turned:
                return turned_ref[i * turned + t]
            return held_ref[first + t].T

        pieces = forward_group(panel_ref, cols_ref, col_base, block_at, lambda t: False, first, unroll)
        add_group(pieces, rows_ref, first, row_base, (acc_a, acc_b))
        return carry

    lax.fori_loop(0, total // unroll, step, 0)
    split_halves((acc_a, acc_b), lax.axis_index("dst") % 2, keep_ref, send_ref)


def adjoint_kernel(unroll, n_src, rows_ref, cols_ref, counts_ref, held_ref, mine_ref, other_ref, *refs):
    keep_ref, send_refs = refs[0], refs[1:n_src]
    panel_ref, acc_a, acc_b = refs[n_src:]
    core = lax.axis_index("dst") % 2
    source = lax.axis_index("src")
    row_base = source * panel_ref.shape[0]
    col_base = lax.axis_index("dst") * acc_a.shape[0]
    half = mine_ref.shape[0]
    panel_ref[pl.ds(core * half, half)] = mine_ref[...]
    panel_ref[pl.ds((1 - core) * half, half)] = other_ref[...]
    acc_a[...] = jnp.zeros_like(acc_a)
    acc_b[...] = jnp.zeros_like(acc_b)

    def step(i, carry):
        first = i * unroll
        pieces = adjoint_group(panel_ref, rows_ref, row_base, held_ref, first, unroll)
        add_group(pieces, cols_ref, first, col_base, (acc_a, acc_b))
        return carry

    lax.fori_loop(0, rows_ref.shape[0] // unroll, step, 0)
    size = keep_ref.shape[0]
    for k in range(n_src):
        span = pl.ds((source ^ k) * size, size)
        scale = jnp.sqrt(counts_ref[span].astype(F32))
        value = (acc_a[span] + acc_b[span]) / scale
        if k == 0:
            keep_ref[...] = value
        else:
            send_refs[k - 1][...] = value.astype(BF16)


def gram_kernel(n_src, last, counts_ref, *refs):
    chunk_refs, (w_ref, gram_ref) = refs[:n_src], refs[n_src:]
    source = lax.axis_index("src")
    size = chunk_refs[0].shape[0]
    for k in range(n_src):
        w_ref[pl.ds((source ^ k) * size, size)] = chunk_refs[k][...]
    wide = jnp.concatenate([w_ref[c] for c in range(w_ref.shape[0])], 1)
    gram_ref[...] = dot_nt(wide, wide)
    if not last:
        w_ref[...] = (w_ref[...].astype(F32) / jnp.sqrt(counts_ref[...].astype(F32))).astype(BF16)


def orth_kernel(box_total, *refs):
    refs[-1][...] = orth_of(refs[:-1], box_total)


def basis_kernel(box_total, w_ref, *refs):
    matrix = orth_of(refs[:-1], box_total)
    side = matrix.shape[0]
    wide = jnp.concatenate([w_ref[c] for c in range(w_ref.shape[0])], 1)
    out = dot_nn(jnp.concatenate(split3(matrix), 0), wide)
    refs[-1][...] = out[:side] + out[side : 2 * side] + out[2 * side :]


def mix_kernel(matrix_ref, scale_ref, keep_ref, core_ref, *refs):
    out_ref = refs[-1]
    half, side, box = out_ref.shape
    total = keep_ref[...] + core_ref[...].astype(F32)
    for ref in refs[:-1]:
        total = total + ref[...].astype(F32)
    wide = jnp.concatenate([total[c] for c in range(half)], 1)
    top, mid, low = split3(wide)
    left = split3(matrix_ref[...])
    one = dot_nn(jnp.concatenate(left, 0), top)
    two = dot_nn(jnp.concatenate(left[:2], 0), mid)
    three = dot_nn(left[0], low)
    mixed = one[:side] + (one[side : 2 * side] + two[:side]) + (one[2 * side :] + two[side:] + three)
    for c in range(half):
        out_ref[c] = (mixed[:, c * box : (c + 1) * box] / scale_ref[c].astype(F32)).astype(BF16)


def swap(x, axis, bits):
    size = lax.axis_size(axis)
    return lax.ppermute(x, axis, [(i, i ^ bits) for i in range(size)])


def per_device(blocks, block_rows, block_cols, row_counts, col_counts, start_panel):
    total, box, _ = blocks.shape
    side = start_panel.shape[0]
    row_blocks = row_counts.shape[0] // box
    col_blocks = col_counts.shape[0] // box
    n_src, n_dst = lax.axis_size("src"), lax.axis_size("dst")
    box_total = float(col_blocks * box * n_dst)
    unroll = unroll_of(total, SECOND)
    first_unroll = unroll_of(total, FIRST)
    turned = unroll * TURNED // 8 // 2 * 2
    half = row_blocks // 2
    size = col_blocks // n_src
    wide_counts = col_counts.reshape(1, col_blocks * box)
    tall_counts = col_counts.reshape(col_blocks, 1, box)
    core = lax.axis_index("dst") % 2
    row_scale = row_counts.reshape(2, half, 1, box)[core]
    forward_cost = cost(2 * total * box * box * 512)
    adjoint_cost = cost(2 * total * box * box * 256)
    small_cost = cost(1 << 28)
    orth_cost = cost(1 << 32)

    keep_out = jax.ShapeDtypeStruct((half, side, box), F32)
    send_out = jax.ShapeDtypeStruct((half, side, box), BF16)
    square = jax.ShapeDtypeStruct((side, side), F32)
    accs = [pltpu.VMEM((row_blocks, side, box), F32)] * 2
    w_full, grams = None, None
    for sweep in range(ITERS):
        if sweep == 0:
            slots = min(total // first_unroll, SLOTS)
            keep, send = pl.pallas_call(
                functools.partial(first_forward_kernel, first_unroll),
                in_specs=[HBM] * 5,
                out_specs=[VMEM, VMEM],
                out_shape=[keep_out, send_out],
                scratch_shapes=[
                    pltpu.SMEM(block_rows.shape, jnp.int32),
                    pltpu.SMEM(block_cols.shape, jnp.int32),
                    pltpu.VMEM(start_panel.shape, F32),
                    pltpu.VMEM(wide_counts.shape, jnp.int32),
                    pltpu.VMEM((slots, first_unroll, box, box), BF16),
                    pltpu.VMEM((col_blocks, side, box), BF16),
                    *accs,
                    pltpu.SemaphoreType.DMA((slots,)),
                    pltpu.SemaphoreType.DMA((4,)),
                ],
                compiler_params=params(22),
                name="first_forward",
                cost_estimate=forward_cost,
            )(*[
                pltpu.with_memory_space_constraint(x, pltpu.HBM)
                for x in (block_rows, block_cols, start_panel, wide_counts, blocks)
            ])
        else:
            keep, send = pl.pallas_call(
                functools.partial(forward_kernel, unroll, turned),
                in_specs=[SMEM, SMEM, VMEM, VMEM, VMEM],
                out_specs=[VMEM, VMEM],
                out_shape=[keep_out, send_out],
                scratch_shapes=accs,
                compiler_params=params(12),
                name="forward",
                cost_estimate=forward_cost,
            )(block_rows, block_cols, held, flipped, w_full)
        core_got = swap(send, "dst", 1)
        if sweep == 0:
            again, core_got = lax.optimization_barrier((blocks, core_got))
            held = pl.pallas_call(
                load_kernel,
                in_specs=[HBM],
                out_specs=VMEM,
                out_shape=pltpu.VMEM(blocks.shape, BF16),
                scratch_shapes=[pltpu.SemaphoreType.DMA],
                compiler_params=params(2),
                name="load",
                cost_estimate=cost(0, 2 * total * box * box * 2),
            )(pltpu.with_memory_space_constraint(again, pltpu.HBM))
        summed = keep + core_got.astype(F32)
        x_got = []
        bits = 2
        while bits < n_dst:
            x_got.append(swap(summed.astype(BF16), "dst", bits))
            summed = summed + x_got[-1].astype(F32)
            bits *= 2
        if sweep == 0:
            summed, held = lax.optimization_barrier((summed, held))
            mine = (summed / row_scale.astype(F32)).astype(BF16)
        else:
            matrix = pl.pallas_call(
                functools.partial(orth_kernel, box_total),
                in_specs=[VMEM] * n_dst,
                out_specs=VMEM,
                out_shape=square,
                compiler_params=params(),
                name="orth",
                cost_estimate=orth_cost,
            )(*grams)
            mine = pl.pallas_call(
                mix_kernel,
                in_specs=[VMEM] * (4 + len(x_got)),
                out_specs=VMEM,
                out_shape=send_out,
                compiler_params=params(),
                name="mix",
                cost_estimate=small_cost,
            )(matrix, row_scale, keep, core_got, *x_got)
        other = swap(mine, "dst", 1)
        chunk = (size, side, box)
        outs = pl.pallas_call(
            functools.partial(adjoint_kernel, unroll_of(total, BACK), n_src),
            in_specs=[SMEM, SMEM] + [VMEM] * 4,
            out_specs=[VMEM] * n_src,
            out_shape=[jax.ShapeDtypeStruct(chunk, F32)]
            + [jax.ShapeDtypeStruct(chunk, BF16)] * (n_src - 1),
            scratch_shapes=[
                pltpu.VMEM((row_blocks, side, box), BF16),
                pltpu.VMEM((col_blocks, side, box), F32),
                pltpu.VMEM((col_blocks, side, box), F32),
            ],
            compiler_params=params(12),
            name="adjoint",
                cost_estimate=adjoint_cost,
        )(block_rows, block_cols, tall_counts, held, mine, other)
        outs = list(outs)
        got = [swap(outs[k], "src", k) for k in range(1, n_src)]
        if sweep == 0:
            outs[0], again = lax.optimization_barrier((outs[0], held))
            flipped = pl.pallas_call(
                functools.partial(turn_kernel, unroll, turned),
                in_specs=[VMEM],
                out_specs=VMEM,
                out_shape=pltpu.VMEM((total // unroll * turned, box, box), BF16),
                compiler_params=params(2),
                name="turn",
                cost_estimate=adjoint_cost,
            )(again)
            got, flipped = lax.optimization_barrier((got, flipped))
        own = tree_sum([outs[0]] + [g.astype(F32) for g in got]).astype(BF16)
        chunks = [own] + [swap(own, "src", k) for k in range(1, n_src)]
        w_full, gram = pl.pallas_call(
            functools.partial(gram_kernel, n_src, sweep == ITERS - 1),
            in_specs=[VMEM] * (1 + n_src),
            out_specs=[VMEM, VMEM],
            out_shape=[jax.ShapeDtypeStruct((col_blocks, side, box), BF16), square],
            compiler_params=params(),
            name="gram",
                cost_estimate=small_cost,
        )(tall_counts, *chunks)
        grams = [gram] + [swap(gram, "dst", k) for k in range(1, n_dst)]
    return pl.pallas_call(
        functools.partial(basis_kernel, box_total),
        in_specs=[VMEM] * (1 + n_dst),
        out_specs=VMEM,
        out_shape=jax.ShapeDtypeStruct((side, col_blocks * box), F32),
        compiler_params=params(),
        name="basis",
                cost_estimate=orth_cost,
    )(w_full, *grams)


def solution(mesh):
    return jax.shard_map(
        per_device,
        mesh=mesh,
        in_specs=(
            P(("groups", "src", "dst"), None, None),
            P(("groups", "src", "dst")),
            P(("groups", "src", "dst")),
            P(("groups", "src")),
            P(("groups", "dst")),
            P(None, ("groups", "dst")),
        ),
        out_specs=P(None, ("groups", "dst")),
        check_vma=False,
    )
```

```python
import functools

import jax
import jax.numpy as jnp
from jax import lax
from jax.experimental import pallas as pl
from jax.experimental.pallas import tpu as pltpu
from jax.sharding import PartitionSpec as P

ITERS = 2
TURNED = 3
FIRST = 128
SECOND = 320
BACK = 640
SLOTS = 3
MIX = 8
F32 = jnp.float32
BF16 = jnp.bfloat16
VMEM = pl.BlockSpec(memory_space=pltpu.VMEM)
SMEM = pl.BlockSpec(memory_space=pltpu.SMEM)
HBM = pl.BlockSpec(memory_space=pltpu.HBM)


def cost(flops, moved=0):
    return pl.CostEstimate(flops=flops, bytes_accessed=moved, transcendentals=0)


def params(mebibytes=6):
    return pltpu.CompilerParams(vmem_limit_bytes=mebibytes << 20)


def dot_nn(a, b, precision=None):
    return lax.dot_general(
        a, b, (((1,), (0,)), ((), ())), preferred_element_type=F32, precision=precision
    )


def dot_nt(a, b, precision=None):
    return lax.dot_general(
        a, b, (((1,), (1,)), ((), ())), preferred_element_type=F32, precision=precision
    )


def unroll_of(total, most):
    return max(size for size in range(8, most + 1, 8) if total % size == 0)


def add_group(pieces, ids_ref, first, base, accs):
    for t, piece in enumerate(pieces):
        acc = accs[t % len(accs)]
        place = ids_ref[first + t] - base
        acc[place] += piece


def forward_group(panel_ref, cols_ref, col_base, block_at, plain, first, size):
    pieces = []
    side, box = panel_ref.shape[1:]
    for t in range(0, size, 2):
        left = jnp.concatenate(
            [
                panel_ref[cols_ref[first + t] - col_base],
                panel_ref[cols_ref[first + t + 1] - col_base],
            ],
            0,
        )
        one, two = block_at(t), block_at(t + 1)
        if plain(t):
            out = dot_nt(left, jnp.concatenate([one, two], 0))
        else:
            out = dot_nn(left, jnp.concatenate([one, two], 1))
        pieces += [out[:side, :box], out[side:, box:]]
    return pieces


def adjoint_group(panel_ref, rows_ref, row_base, held_ref, first, size):
    pieces = []
    side, box = panel_ref.shape[1:]
    for t in range(0, size, 2):
        left = jnp.concatenate(
            [
                panel_ref[rows_ref[first + t] - row_base],
                panel_ref[rows_ref[first + t + 1] - row_base],
            ],
            0,
        )
        right = jnp.concatenate([held_ref[first + t], held_ref[first + t + 1]], 1)
        out = dot_nn(left, right)
        pieces += [out[:side, :box], out[side:, box:]]
    return pieces


def inverse_factor(gram):
    side = gram.shape[0]
    row = lax.broadcasted_iota(jnp.int32, (side, 2 * side), 0)
    col = lax.broadcasted_iota(jnp.int32, (side, 2 * side), 1)
    work = jnp.concatenate([gram, jnp.zeros_like(gram)], 1) + (col == row + side).astype(F32)
    for j in range(0, side, 4):
        column = [jnp.broadcast_to(work[:, j + k : j + k + 1], work.shape) for k in range(4)]
        r0, r1, r2, r3 = [work[j + k : j + k + 1, :] for k in range(4)]
        at = [[column[k][j + i : j + i + 1, :] for k in range(4)] for i in range(4)]
        a, b, c = at[0][0], at[1][0], at[1][1]
        inv = 1.0 / (a * c - b * b)
        ia, ib, ic = c * inv, -b * inv, a * inv
        t0, t1 = ia * r0 + ib * r1, ib * r0 + ic * r1
        p0, p1, q0, q1 = at[2][0], at[2][1], at[3][0], at[3][1]
        gp0, gp1 = ia * p0 + ib * p1, ib * p0 + ic * p1
        gq0, gq1 = ia * q0 + ib * q1, ib * q0 + ic * q1
        sa = at[2][2] - (p0 * gp0 + p1 * gp1)
        sb = at[3][2] - (q0 * gp0 + q1 * gp1)
        sc = at[3][3] - (q0 * gq0 + q1 * gq1)
        n1 = r1 - (b / a) * r0
        n2 = r2 - (p0 * t0 + p1 * t1)
        n3 = r3 - (q0 * t0 + q1 * t1)
        inv_s = 1.0 / (sa * sc - sb * sb)
        u0, u1 = (sc * n2 - sb * n3) * inv_s, (sa * n3 - sb * n2) * inv_s
        v0, v1 = t0 - (gp0 * u0 + gq0 * u1), t1 - (gp1 * u0 + gq1 * u1)
        below = work - ((column[0] * v0 + column[1] * v1) + (column[2] * u0 + column[3] * u1))
        work = jnp.where(row > j + 3, below, work)
        for k, new in ((1, n1), (2, n2), (3, n3 - (sb / sa) * n2)):
            work = jnp.where(row == j + k, new, work)
    diag = jnp.sum(jnp.where(col == row, work, 0.0), axis=1, keepdims=True)
    return work[:, side:] / jnp.sqrt(diag)


def orth_matrix(gram):
    first = inverse_factor(gram)
    high = lax.Precision.HIGHEST
    again = dot_nt(dot_nn(first, gram, high), first, high)
    return dot_nn(inverse_factor(again), first, high)


def tree_sum(parts):
    while len(parts) > 1:
        parts = [parts[i] + parts[i + 1] for i in range(0, len(parts), 2)]
    return parts[0]


def split3(x):
    top = x.astype(BF16)
    rest = x - top.astype(F32)
    mid = rest.astype(BF16)
    return top, mid, (rest - mid.astype(F32)).astype(BF16)


def orth_of(gram_refs, box_total):
    return orth_matrix(tree_sum([g[...] for g in gram_refs]) / box_total)


def store_scaled(basis, counts_ref, panel_ref):
    box = panel_ref.shape[2]
    scaled = (basis / jnp.sqrt(counts_ref[...].astype(F32))).astype(BF16)
    for c in range(panel_ref.shape[0]):
        panel_ref[c] = scaled[:, c * box : (c + 1) * box]


def split_halves(accs, core, keep_ref, send_ref):
    half = keep_ref.shape[0]
    mine = pl.ds(core * half, half)
    other = pl.ds((1 - core) * half, half)
    keep_ref[...] = functools.reduce(jnp.add, [a[mine] for a in accs])
    send_ref[...] = functools.reduce(jnp.add, [a[other] for a in accs]).astype(BF16)


def first_forward_kernel(
    unroll, rows_hbm, cols_hbm, start_hbm, counts_hbm, blocks_hbm,
    keep_ref, send_ref,
    rows_ref, cols_ref, start_ref, counts_ref, blocks_ref, panel_ref, acc_a, acc_b, sems, small_sems,
):
    steps = blocks_hbm.shape[0] // unroll
    slots = blocks_ref.shape[0]

    def part(i, slot):
        return pltpu.make_async_copy(
            blocks_hbm.at[pl.ds(i * unroll, unroll)], blocks_ref.at[slot], sems.at[slot]
        )

    small = [
        pltpu.make_async_copy(source, target, small_sems.at[i])
        for i, (source, target) in enumerate(
            (
                (start_hbm, start_ref),
                (counts_hbm, counts_ref),
                (rows_hbm, rows_ref),
                (cols_hbm, cols_ref),
            )
        )
    ]
    for copy in small:
        copy.start()
    for i in range(min(slots, steps)):
        part(i, i).start()
    row_base = lax.axis_index("src") * acc_a.shape[0]
    col_base = lax.axis_index("dst") * panel_ref.shape[0]
    acc_a[...] = jnp.zeros_like(acc_a)
    acc_b[...] = jnp.zeros_like(acc_b)
    for copy in small:
        copy.wait()
    store_scaled(start_ref[...], counts_ref, panel_ref)

    def step(i, carry):
        slot = lax.rem(i, slots)
        part(i, slot).wait()

        def plain(t):
            return t % MIX == MIX - 2

        def block_at(t):
            block = blocks_ref[slot, t]
            return block if plain(t // 2 * 2) else block.T

        pieces = forward_group(
            panel_ref, cols_ref, col_base, block_at, plain, i * unroll, unroll
        )
        add_group(pieces, rows_ref, i * unroll, row_base, (acc_a, acc_b))

        @pl.when(i + slots < steps)
        def _():
            part(i + slots, slot).start()

        return carry

    lax.fori_loop(0, steps, step, 0)
    split_halves((acc_a, acc_b), lax.axis_index("dst") % 2, keep_ref, send_ref)


def load_kernel(hbm_ref, held_ref, sem):
    copy = pltpu.make_async_copy(hbm_ref, held_ref, sem)
    copy.start()
    copy.wait()


def turn_kernel(unroll, turned, held_ref, turned_ref):
    for i in range(turned_ref.shape[0] // turned):
        for t in range(turned):
            turned_ref[i * turned + t] = held_ref[i * unroll + t].T


def forward_kernel(unroll, turned, rows_ref, cols_ref, held_ref, turned_ref, panel_ref, keep_ref, send_ref, acc_a, acc_b):
    total = rows_ref.shape[0]
    row_base = lax.axis_index("src") * acc_a.shape[0]
    col_base = lax.axis_index("dst") * panel_ref.shape[0]
    acc_a[...] = jnp.zeros_like(acc_a)
    acc_b[...] = jnp.zeros_like(acc_b)

    def step(i, carry):
        first = i * unroll

        def block_at(t):
            if t < turned:
                return turned_ref[i * turned + t]
            return held_ref[first + t].T

        pieces = forward_group(panel_ref, cols_ref, col_base, block_at, lambda t: False, first, unroll)
        add_group(pieces, rows_ref, first, row_base, (acc_a, acc_b))
        return carry

    lax.fori_loop(0, total // unroll, step, 0)
    split_halves((acc_a, acc_b), lax.axis_index("dst") % 2, keep_ref, send_ref)


def adjoint_kernel(unroll, n_src, rows_ref, cols_ref, counts_ref, held_ref, mine_ref, other_ref, *refs):
    keep_ref, send_refs = refs[0], refs[1:n_src]
    panel_ref, acc_a, acc_b = refs[n_src:]
    core = lax.axis_index("dst") % 2
    source = lax.axis_index("src")
    row_base = source * panel_ref.shape[0]
    col_base = lax.axis_index("dst") * acc_a.shape[0]
    half = mine_ref.shape[0]
    panel_ref[pl.ds(core * half, half)] = mine_ref[...]
    panel_ref[pl.ds((1 - core) * half, half)] = other_ref[...]
    acc_a[...] = jnp.zeros_like(acc_a)
    acc_b[...] = jnp.zeros_like(acc_b)

    def step(i, carry):
        first = i * unroll
        pieces = adjoint_group(panel_ref, rows_ref, row_base, held_ref, first, unroll)
        add_group(pieces, cols_ref, first, col_base, (acc_a, acc_b))
        return carry

    lax.fori_loop(0, rows_ref.shape[0] // unroll, step, 0)
    size = keep_ref.shape[0]
    for k in range(n_src):
        span = pl.ds((source ^ k) * size, size)
        scale = jnp.sqrt(counts_ref[span].astype(F32))
        value = (acc_a[span] + acc_b[span]) / scale
        if k == 0:
            keep_ref[...] = value
        else:
            send_refs[k - 1][...] = value.astype(BF16)


def gram_kernel(n_src, last, counts_ref, *refs):
    chunk_refs, (w_ref, gram_ref) = refs[:n_src], refs[n_src:]
    source = lax.axis_index("src")
    size = chunk_refs[0].shape[0]
    for k in range(n_src):
        w_ref[pl.ds((source ^ k) * size, size)] = chunk_refs[k][...]
    wide = jnp.concatenate([w_ref[c] for c in range(w_ref.shape[0])], 1)
    gram_ref[...] = dot_nt(wide, wide)
    if not last:
        w_ref[...] = (w_ref[...].astype(F32) / jnp.sqrt(counts_ref[...].astype(F32))).astype(BF16)


def orth_kernel(box_total, *refs):
    refs[-1][...] = orth_of(refs[:-1], box_total)


def basis_kernel(box_total, w_ref, *refs):
    matrix = orth_of(refs[:-1], box_total)
    side = matrix.shape[0]
    wide = jnp.concatenate([w_ref[c] for c in range(w_ref.shape[0])], 1)
    out = dot_nn(jnp.concatenate(split3(matrix), 0), wide)
    refs[-1][...] = out[:side] + out[side : 2 * side] + out[2 * side :]


def mix_kernel(matrix_ref, scale_ref, keep_ref, core_ref, *refs):
    out_ref = refs[-1]
    half, side, box = out_ref.shape
    total = keep_ref[...] + core_ref[...].astype(F32)
    for ref in refs[:-1]:
        total = total + ref[...].astype(F32)
    wide = jnp.concatenate([total[c] for c in range(half)], 1)
    top, mid, low = split3(wide)
    left = split3(matrix_ref[...])
    one = dot_nn(jnp.concatenate(left, 0), top)
    two = dot_nn(jnp.concatenate(left[:2], 0), mid)
    three = dot_nn(left[0], low)
    mixed = one[:side] + (one[side : 2 * side] + two[:side]) + (one[2 * side :] + two[side:] + three)
    for c in range(half):
        out_ref[c] = (mixed[:, c * box : (c + 1) * box] / scale_ref[c].astype(F32)).astype(BF16)


def swap(x, axis, bits):
    size = lax.axis_size(axis)
    return lax.ppermute(x, axis, [(i, i ^ bits) for i in range(size)])


def per_device(blocks, block_rows, block_cols, row_counts, col_counts, start_panel):
    total, box, _ = blocks.shape
    side = start_panel.shape[0]
    row_blocks = row_counts.shape[0] // box
    col_blocks = col_counts.shape[0] // box
    n_src, n_dst = lax.axis_size("src"), lax.axis_size("dst")
    box_total = float(col_blocks * box * n_dst)
    unroll = unroll_of(total, SECOND)
    first_unroll = unroll_of(total, FIRST)
    turned = unroll * TURNED // 8 // 2 * 2
    half = row_blocks // 2
    size = col_blocks // n_src
    wide_counts = col_counts.reshape(1, col_blocks * box)
    tall_counts = col_counts.reshape(col_blocks, 1, box)
    core = lax.axis_index("dst") % 2
    row_scale = row_counts.reshape(2, half, 1, box)[core]
    forward_cost = cost(2 * total * box * box * 512)
    adjoint_cost = cost(2 * total * box * box * 256)
    small_cost = cost(1 << 28)
    orth_cost = cost(1 << 32)

    keep_out = jax.ShapeDtypeStruct((half, side, box), F32)
    send_out = jax.ShapeDtypeStruct((half, side, box), BF16)
    square = jax.ShapeDtypeStruct((side, side), F32)
    accs = [pltpu.VMEM((row_blocks, side, box), F32)] * 2
    w_full, grams = None, None
    for sweep in range(ITERS):
        if sweep == 0:
            slots = min(total // first_unroll, SLOTS)
            keep, send = pl.pallas_call(
                functools.partial(first_forward_kernel, first_unroll),
                in_specs=[HBM] * 5,
                out_specs=[VMEM, VMEM],
                out_shape=[keep_out, send_out],
                scratch_shapes=[
                    pltpu.SMEM(block_rows.shape, jnp.int32),
                    pltpu.SMEM(block_cols.shape, jnp.int32),
                    pltpu.VMEM(start_panel.shape, F32),
                    pltpu.VMEM(wide_counts.shape, jnp.int32),
                    pltpu.VMEM((slots, first_unroll, box, box), BF16),
                    pltpu.VMEM((col_blocks, side, box), BF16),
                    *accs,
                    pltpu.SemaphoreType.DMA((slots,)),
                    pltpu.SemaphoreType.DMA((4,)),
                ],
                compiler_params=params(22),
                name="first_forward",
                cost_estimate=forward_cost,
            )(*[
                pltpu.with_memory_space_constraint(x, pltpu.HBM)
                for x in (block_rows, block_cols, start_panel, wide_counts, blocks)
            ])
        else:
            keep, send = pl.pallas_call(
                functools.partial(forward_kernel, unroll, turned),
                in_specs=[SMEM, SMEM, VMEM, VMEM, VMEM],
                out_specs=[VMEM, VMEM],
                out_shape=[keep_out, send_out],
                scratch_shapes=accs,
                compiler_params=params(24),
                name="forward",
                cost_estimate=forward_cost,
            )(block_rows, block_cols, held, flipped, w_full)
        core_got = swap(send, "dst", 1)
        if sweep == 0:
            again, core_got = lax.optimization_barrier((blocks, core_got))
            held = pl.pallas_call(
                load_kernel,
                in_specs=[HBM],
                out_specs=VMEM,
                out_shape=pltpu.VMEM(blocks.shape, BF16),
                scratch_shapes=[pltpu.SemaphoreType.DMA],
                compiler_params=params(2),
                name="load",
                cost_estimate=cost(0, 2 * total * box * box * 2),
            )(pltpu.with_memory_space_constraint(again, pltpu.HBM))
        summed = keep + core_got.astype(F32)
        x_got = []
        bits = 2
        while bits < n_dst:
            x_got.append(swap(summed.astype(BF16), "dst", bits))
            summed = summed + x_got[-1].astype(F32)
            bits *= 2
        if sweep == 0:
            summed, held = lax.optimization_barrier((summed, held))
            mine = (summed / row_scale.astype(F32)).astype(BF16)
        else:
            matrix = pl.pallas_call(
                functools.partial(orth_kernel, box_total),
                in_specs=[VMEM] * n_dst,
                out_specs=VMEM,
                out_shape=square,
                compiler_params=params(),
                name="orth",
                cost_estimate=orth_cost,
            )(*grams)
            mine = pl.pallas_call(
                mix_kernel,
                in_specs=[VMEM] * (4 + len(x_got)),
                out_specs=VMEM,
                out_shape=send_out,
                compiler_params=params(),
                name="mix",
                cost_estimate=small_cost,
            )(matrix, row_scale, keep, core_got, *x_got)
        other = swap(mine, "dst", 1)
        chunk = (size, side, box)
        outs = pl.pallas_call(
            functools.partial(adjoint_kernel, unroll_of(total, BACK), n_src),
            in_specs=[SMEM, SMEM] + [VMEM] * 4,
            out_specs=[VMEM] * n_src,
            out_shape=[jax.ShapeDtypeStruct(chunk, F32)]
            + [jax.ShapeDtypeStruct(chunk, BF16)] * (n_src - 1),
            scratch_shapes=[
                pltpu.VMEM((row_blocks, side, box), BF16),
                pltpu.VMEM((col_blocks, side, box), F32),
                pltpu.VMEM((col_blocks, side, box), F32),
            ],
            compiler_params=params(24),
            name="adjoint",
                cost_estimate=adjoint_cost,
        )(block_rows, block_cols, tall_counts, held, mine, other)
        outs = list(outs)
        got = [swap(outs[k], "src", k) for k in range(1, n_src)]
        if sweep == 0:
            outs[0], again = lax.optimization_barrier((outs[0], held))
            flipped = pl.pallas_call(
                functools.partial(turn_kernel, unroll, turned),
                in_specs=[VMEM],
                out_specs=VMEM,
                out_shape=pltpu.VMEM((total // unroll * turned, box, box), BF16),
                compiler_params=params(2),
                name="turn",
                cost_estimate=adjoint_cost,
            )(again)
            got, flipped = lax.optimization_barrier((got, flipped))
        own = tree_sum([outs[0]] + [g.astype(F32) for g in got]).astype(BF16)
        chunks = [own] + [swap(own, "src", k) for k in range(1, n_src)]
        w_full, gram = pl.pallas_call(
            functools.partial(gram_kernel, n_src, sweep == ITERS - 1),
            in_specs=[VMEM] * (1 + n_src),
            out_specs=[VMEM, VMEM],
            out_shape=[jax.ShapeDtypeStruct((col_blocks, side, box), BF16), square],
            compiler_params=params(),
            name="gram",
                cost_estimate=small_cost,
        )(tall_counts, *chunks)
        grams = [gram] + [swap(gram, "dst", k) for k in range(1, n_dst)]
    return pl.pallas_call(
        functools.partial(basis_kernel, box_total),
        in_specs=[VMEM] * (1 + n_dst),
        out_specs=VMEM,
        out_shape=jax.ShapeDtypeStruct((side, col_blocks * box), F32),
        compiler_params=params(),
        name="basis",
                cost_estimate=orth_cost,
    )(w_full, *grams)


def solution(mesh):
    return jax.shard_map(
        per_device,
        mesh=mesh,
        in_specs=(
            P(("groups", "src", "dst"), None, None),
            P(("groups", "src", "dst")),
            P(("groups", "src", "dst")),
            P(("groups", "src")),
            P(("groups", "dst")),
            P(None, ("groups", "dst")),
        ),
        out_specs=P(None, ("groups", "dst")),
        check_vma=False,
    )
```
